32 devices in a mesh: rows: 16 (over z, y, x), cols: 2 (over core).
Axes of the slice: x: 2, y: 2, z: 4, core: 2. Of those that a mesh axis runs over, the one named last changes fastest.
Arguments:
- queries: bfloat16 [8192, 128], P('rows'), may hold values from -1 to 1
- prototypes: bfloat16 [16384, 128], P('cols'), may hold values from -1 to 1
- potential: float32 [16384], P('cols'), may hold values from -0.15 to 0.15
- weights: int32 [8192], P('rows'), may hold values from 1 to 10, as said below
- capacity: int32 [16384], P('cols'), may hold values from 1 to 7, as said below
- cotangent: bfloat16 [8192, 128], P('rows'), may hold values from -16 to 16
Outputs:
- grad_queries: float32 [8192, 128], P(('rows', 'cols'))
- grad_protos: float32 [16384, 128], P('cols')
The draws below stay inside these ranges and needn't reach their ends.
Inputs may be any that keep to these rules, and one draw needn't show every extreme that they name: weights rise along the queries: the first quarter are all 1, the k-th quarter (k = 0..3) lies in 1 + k to 1 + 3 k. `capacity`: capacities rise along the slots: the k-th quarter (k = 0..3) lies in 1 + k to 1 + 2 k.
All inputs are finite; a program needn't handle non-finite values.
Results may differ from the reference program's by a relative error of at most 0.0019.
The reference program's roundings to bfloat16 on the way (of `qhat`, `phat` and `scaled`) count: a program that leaves them out, or rounds other values in their place, can miss the bound.
Values sent between devices are 32-bit elements; how exact they have to be, the bound alone decides.
A program may use at most 128 MiB of HBM per device.

```python
import math
import jax
import jax.numpy as jnp
from jax import lax

F = 128
NS = 16384
NQ = 8192


def draw_weights(key, part):
    index = jnp.arange(NQ, dtype=jnp.int32)
    level = 4 * index // NQ
    return jax.random.randint(jax.random.fold_in(key, 11), (NQ,), 1 + level, 2 + 3 * level, dtype=jnp.int32)


def draw_capacity(key, part):
    index = jnp.arange(NS, dtype=jnp.int32)
    level = 4 * index // NS
    return jax.random.randint(jax.random.fold_in(key, 23), (NS,), 1 + level, 2 + 2 * level, dtype=jnp.int32)


def harmonic_rows(bearing, radius, jitter):
    columns = [radius * jnp.cos(bearing), radius * jnp.sin(bearing)]
    for harmonic in range(2, 6):
        columns.append(0.15 * jnp.cos(harmonic * bearing))
        columns.append(0.15 * jnp.sin(harmonic * bearing))
    signal = jnp.stack(columns, axis=1)
    signal = jnp.pad(signal, ((0, 0), (0, jitter.shape[1] - 10)))
    return jnp.clip(signal + jitter, -1.0, 1.0)


def draw_queries(key, part):
    subkeys = jax.random.split(jax.random.fold_in(key, 41), 3)
    bearing = jax.random.uniform(subkeys[0], (NQ,), jnp.float32, -jnp.pi, jnp.pi)
    radius = jax.random.uniform(subkeys[1], (NQ,), jnp.float32, 0.55, 1.1)
    jitter = jax.random.normal(subkeys[2], (NQ, F), jnp.float32) * (0.5 / F) ** 0.5
    return harmonic_rows(bearing, radius, jitter).astype(jnp.bfloat16)


def draw_prototypes(key, part):
    subkeys = jax.random.split(jax.random.fold_in(key, 43), 3)
    bearing = jax.random.uniform(subkeys[0], (NS,), jnp.float32, -jnp.pi, jnp.pi)
    radius = jax.random.uniform(subkeys[1], (NS,), jnp.float32, 0.55, 1.1)
    jitter = jax.random.normal(subkeys[2], (NS, F), jnp.float32) * (0.5 / F) ** 0.5
    return harmonic_rows(bearing, radius, jitter).astype(jnp.bfloat16)


def draw_cotangent(key, part):
    subkeys = jax.random.split(jax.random.fold_in(key, 47), 2)
    polarity = 2.0 * jax.random.randint(subkeys[0], (8,), 0, 2).astype(jnp.float32) - 1.0
    strength = 3.0
    jitter = jax.random.normal(subkeys[1], (NQ, F), jnp.float32) * 4.0
    offset = jnp.concatenate([jnp.zeros((2,), jnp.float32), strength * polarity, jnp.zeros((F - 10,), jnp.float32)])
    return jnp.clip(jitter + offset[None, :], -16.0, 16.0).astype(jnp.bfloat16)


def level_of(stream_key, extent, cuts, least, high):
    level = 1.0
    for axis_at, parts in cuts:
        heights = jax.random.uniform(jax.random.fold_in(jax.random.fold_in(stream_key, 6), axis_at), (parts,), jnp.float32, least / len(cuts), high / len(cuts))
        level = level * jnp.repeat(jnp.exp(heights), extent[axis_at] // parts).reshape((-1,) + (1,) * (len(extent) - 1 - axis_at))
    return level


def setup_inputs(seed: int = 0) -> dict:
    streams_of = jax.random.split(jax.random.key(seed), 7)
    return {
        "queries": draw_queries(jax.random.fold_in(streams_of[6], 71), 0),
        "prototypes": draw_prototypes(jax.random.fold_in(streams_of[6], 71), 0),
        "potential": jnp.clip(jax.random.uniform(streams_of[2], (NS,), jnp.float32, -0.15, 0.15) * level_of(streams_of[2], (NS,), ((0, 2),), -0.4, 0.0), -0.15, 0.15),
        "weights": draw_weights(jax.random.fold_in(streams_of[6], 71), 0),
        "capacity": draw_capacity(jax.random.fold_in(streams_of[6], 71), 0),
        "cotangent": draw_cotangent(jax.random.fold_in(streams_of[6], 71), 0),
    }


TEMPER = 0.05

def unit_rows(matrix):
    wide = matrix.astype(jnp.float32)
    length = jnp.sqrt(lax.optimization_barrier(jnp.sum(wide * wide, axis=1)) + 1e-06)
    return ((wide / length[:, None]).astype(jnp.bfloat16), length)

def unit_back(grad, unit, length):
    wide = unit.astype(jnp.float32)
    along = lax.optimization_barrier(jnp.sum(wide * grad, axis=1, keepdims=True))
    return (grad - wide * along) / length[:, None]

def pair_dot(left, right):
    return lax.dot_general(left, right, (((1,), (1,)), ((), ())), preferred_element_type=jnp.float32)

def kernel_tile(qrows, phat, potential, capacity):
    scores = pair_dot(qrows, phat)
    return capacity.astype(jnp.float32)[None, :] * jnp.exp((scores - potential[None, :]) / TEMPER)

def reference(queries, prototypes, potential, weights, capacity, cotangent):
    qhat, qlen = unit_rows(queries)
    phat, plen = unit_rows(prototypes)
    wgt = weights.astype(jnp.float32)
    scaled = (cotangent.astype(jnp.float32) / wgt[:, None]).astype(jnp.bfloat16)
    total = qhat.shape[0]
    feats = qhat.shape[1]
    slots = phat.shape[0]
    block = math.gcd(total, 256)
    count = total // block
    qblocks = qhat.reshape(count, block, feats)
    sblocks = scaled.reshape(count, block, feats)
    wblocks = wgt.reshape(count, block)

    def first(args):
        qrows, srows = args
        kern = kernel_tile(qrows, phat, potential, capacity)
        coupling = pair_dot(srows, phat)
        return (lax.optimization_barrier(jnp.sum(kern, axis=1)), lax.optimization_barrier(jnp.sum(kern * coupling, axis=1)))
    ztot, kgsum = lax.map(first, (qblocks, sblocks))
    share = wblocks / ztot
    pvec = share * kgsum
    alpha_one = pvec / wblocks

    def second(carry, args):
        qrows, srows, srate, arow = args
        kern = kernel_tile(qrows, phat, potential, capacity)
        coupling = pair_dot(srows, phat)
        plan = srate[:, None] * kern
        return ((carry[0] + lax.optimization_barrier(jnp.sum(plan, axis=0)), carry[1] + lax.optimization_barrier(jnp.sum(plan * coupling, axis=0)), carry[2] + lax.optimization_barrier(jnp.sum(arow[:, None] * plan, axis=0))), None)
    empty = jnp.zeros((slots,), jnp.float32)
    (colsum, qvec, t_one), _ = lax.scan(second, (empty, empty, empty), (qblocks, sblocks, share, alpha_one))
    beta_one = (qvec - t_one) / colsum

    def third(args):
        qrows, srate = args
        plan = srate[:, None] * kernel_tile(qrows, phat, potential, capacity)
        return lax.optimization_barrier(jnp.sum(plan * beta_one[None, :], axis=1))
    rowprod = lax.map(third, (qblocks, share))
    alpha_two = (pvec - rowprod) / wblocks

    def fourth(carry, args):
        qrows, srate, arow = args
        plan = srate[:, None] * kernel_tile(qrows, phat, potential, capacity)
        return (carry + lax.optimization_barrier(jnp.sum(arow[:, None] * plan, axis=0)), None)
    t_two, _ = lax.scan(fourth, empty, (qblocks, share, alpha_two))
    beta_two = (qvec - t_two) / colsum

    def fifth(carry, args):
        qrows, srows, srate, arow = args
        kern = kernel_tile(qrows, phat, potential, capacity)
        coupling = pair_dot(srows, phat)
        plan = srate[:, None] * kern
        dscore = (plan * (coupling - arow[:, None] - beta_two[None, :]) / TEMPER).astype(jnp.bfloat16)
        planb = plan.astype(jnp.bfloat16)
        dq = jnp.dot(dscore, phat, preferred_element_type=jnp.float32)
        dp = lax.dot_general(dscore, qrows, (((0,), (0,)), ((), ())), preferred_element_type=jnp.float32)
        dp = dp + lax.dot_general(planb, srows, (((0,), (0,)), ((), ())), preferred_element_type=jnp.float32)
        return (carry + dp, dq)
    dphat, dqhat = lax.scan(fifth, jnp.zeros((slots, feats), jnp.float32), (qblocks, sblocks, share, alpha_two))
    grad_queries = unit_back(dqhat.reshape(total, feats), qhat, qlen)
    grad_protos = unit_back(dphat, phat, plen)
    return (grad_queries, grad_protos)
```

```python
import functools
import math

import jax
import jax.numpy as jnp
from jax import lax
from jax.experimental import pallas as pl
from jax.experimental.pallas import tpu as pltpu
from jax.sharding import PartitionSpec as P

TEMPER = 0.05
LANES = 128
MESH = pl.DeviceIdType.MESH


def unit_rows(matrix):
    wide = matrix.astype(jnp.float32)
    length = jnp.sqrt(jnp.sum(wide * wide, axis=1) + 1e-06)
    return ((wide / length[:, None]).astype(jnp.bfloat16), length)


def unit_back(grad, unit, length):
    wide = unit.astype(jnp.float32)
    along = jnp.sum(wide * grad, axis=1, keepdims=True)
    return (grad - wide * along) / length[:, None]


def nt_dot(left, right):
    return lax.dot_general(
        left, right, (((1,), (1,)), ((), ())), preferred_element_type=jnp.float32
    )


def tiles_of(slots, rows):
    width = max(slots // rows, LANES)
    return width, slots // width


def push(src, dst, send, recv, device):
    return pltpu.make_async_remote_copy(
        src_ref=src, dst_ref=dst, send_sem=send, recv_sem=recv,
        device_id=device, device_id_type=MESH,
    )


def main_kernel(
    rows, cols, qhat, scaled, phat, offset, wgt, left_t, dp_out, dq_out,
    kern, coup, zacc, kacc, share, alpha, cbuf, part, pbuf, beta, gpart, gbuf, shift,
    invs, dqacc, dqbuf,
    csend, crecv, psend, precv, bsend, brecv, rsend, rrecv, gsend, grecv, hsend, hrecv,
    dsend, drecv,
):
    tiles, queries, width = kern.shape
    lanes = [slice(k, k + LANES) for k in range(0, width, LANES)]
    r = lax.axis_index("rows")
    c = lax.axis_index("cols")

    barrier = pltpu.get_barrier_semaphore()
    for o in range(1, rows):
        pl.semaphore_signal(
            barrier, inc=1, device_id=(lax.rem(r + o, rows), c), device_id_type=MESH
        )
    for o in range(1, cols):
        pl.semaphore_signal(
            barrier, inc=1, device_id=(r, lax.rem(c + o, cols)), device_id_type=MESH
        )

    zacc[...] = jnp.zeros_like(zacc)
    kacc[...] = jnp.zeros_like(kacc)
    dqacc[...] = jnp.zeros_like(dqacc)
    log2e = 1.0 / (TEMPER * math.log(2.0))
    step = min(queries, 256)

    def first(t, carry):
        proto = phat[t]
        base = offset[t]
        for q in range(0, queries, step):
            qs = slice(q, q + step)
            k = jnp.exp2(nt_dot(qhat[qs], proto) * log2e + base)
            g = nt_dot(scaled[qs], proto)
            kern[t, qs, :] = k
            coup[t, qs, :] = g
            kg = k * g
            zsum = k[:, lanes[0]]
            gsum = kg[:, lanes[0]]
            for l in lanes[1:]:
                zsum = zsum + k[:, l]
                gsum = gsum + kg[:, l]
            zacc[qs, :] += zsum
            kacc[qs, :] += gsum
        return carry

    lax.fori_loop(0, tiles, first, 0)
    pl.semaphore_wait(barrier, rows - 1 + cols - 1)

    lane = lax.broadcasted_iota(jnp.int32, (queries, LANES), 1)

    def over_cols(send, recv):
        copies = []
        for o in range(1, cols):
            cp = push(
                cbuf.at[0], cbuf.at[o], send.at[o], recv.at[o],
                (r, lax.rem(c + o, cols)),
            )
            cp.start()
            copies.append(cp)
        for cp in copies:
            cp.wait()
        total = cbuf[0]
        for o in range(1, cols):
            total = total + cbuf[o]
        return total

    ztot = jnp.sum(zacc[...], axis=1, keepdims=True)
    kgsum = jnp.sum(kacc[...], axis=1, keepdims=True)
    cbuf[0] = jnp.where(lane == 0, ztot, kgsum)
    total = over_cols(csend, crecv)
    ztot = total[:, 0:1]
    kgsum = total[:, 1:2]
    w = wgt[...]
    srate = w / ztot
    share[...] = jnp.broadcast_to(srate, share.shape)
    alpha[...] = jnp.broadcast_to(srate * kgsum / w, alpha.shape)

    def second(t, carry):
        for l in lanes:
            p = share[...] * kern[t, :, l]
            kern[t, :, l] = p
            part[t, 0:1, l] = jnp.sum(p, axis=0, keepdims=True)
            part[t, 1:2, l] = jnp.sum(
                p * (coup[t, :, l] - alpha[...]), axis=0, keepdims=True
            )
        return carry

    lax.fori_loop(0, tiles, second, 0)

    def scatter(src, dst, send, recv):
        def each(o, carry):
            peer = lax.rem(r + o, rows)

            def go():
                push(src.at[peer], dst.at[o], send.at[o], recv.at[o], (peer, c)).start()

            if tiles == rows:
                go()
            else:
                pl.when(peer < tiles)(go)
            return carry

        lax.fori_loop(1, rows, each, 0)

        def done(o, carry):
            peer = lax.rem(r + o, rows)

            def sent():
                push(src.at[0], dst.at[o], send.at[o], recv.at[o], (peer, c)).wait_send()

            def got():
                push(src.at[0], dst.at[o], send.at[o], recv.at[o], (peer, c)).wait_recv()

            if tiles == rows:
                sent()
                got()
            else:
                pl.when(peer < tiles)(sent)
                pl.when(r < tiles)(got)
            return carry

        lax.fori_loop(1, rows, done, 0)

    def spread(buf, send, recv):
        def each(o, carry):
            peer = lax.rem(r + o, rows)

            def go():
                push(buf.at[r], buf.at[r], send.at[o], recv.at[o], (peer, c)).start()

            if tiles == rows:
                go()
            else:
                pl.when(r < tiles)(go)
            return carry

        lax.fori_loop(1, rows, each, 0)

        def done(o, carry):
            origin = lax.rem(r + rows - o, rows)
            peer = lax.rem(r + o, rows)

            def sent():
                push(buf.at[r], buf.at[r], send.at[o], recv.at[o], (peer, c)).wait_send()

            def got():
                push(
                    buf.at[origin], buf.at[origin], send.at[o], recv.at[o], (peer, c)
                ).wait_recv()

            if tiles == rows:
                sent()
                got()
            else:
                pl.when(r < tiles)(sent)
                pl.when(origin < tiles)(got)
            return carry

        lax.fori_loop(1, rows, done, 0)

    def own(body):
        if tiles == rows:
            body()
        else:
            pl.when(r < tiles)(body)

    scatter(part, pbuf, psend, precv)

    def first_beta():
        both = part[r]
        for o in range(1, rows):
            both = both + pbuf[o]
        inv = 1.0 / both[0:1]
        invs[...] = inv
        beta[r] = both[1:2] * inv

    own(first_beta)
    spread(beta, bsend, brecv)

    zacc[...] = jnp.zeros_like(zacc)

    def third(t, carry):
        acc = zacc[...]
        for l in lanes:
            acc = acc + kern[t, :, l] * beta[t, :, l]
        zacc[...] = acc
        return carry

    lax.fori_loop(0, tiles, third, 0)
    rowprod = jnp.sum(zacc[...], axis=1, keepdims=True)
    cbuf2 = jnp.broadcast_to(rowprod, (queries, LANES))
    kacc[...] = cbuf2
    copies = []
    for o in range(1, cols):
        cp = push(
            kacc, dqbuf.at[o], rsend.at[o], rrecv.at[o], (r, lax.rem(c + o, cols))
        )
        cp.start()
        copies.append(cp)
    for cp in copies:
        cp.wait()
    rowtot = kacc[...]
    for o in range(1, cols):
        rowtot = rowtot + dqbuf[o]
    change = rowtot / w
    share[...] = change
    alpha[...] = alpha[...] - change

    def fourth(t, carry):
        for l in lanes:
            gpart[t, :, l] = jnp.sum(share[...] * kern[t, :, l], axis=0, keepdims=True)
        return carry

    lax.fori_loop(0, tiles, fourth, 0)
    scatter(gpart, gbuf, gsend, grecv)

    def second_beta():
        tot = gpart[r]
        for o in range(1, rows):
            tot = tot + gbuf[o]
        shift[r] = beta[r] + tot * invs[...]

    own(second_beta)
    spread(shift, hsend, hrecv)

    def fifth(t, carry):
        ds = []
        pb = []
        for l in lanes:
            p = kern[t, :, l]
            ds.append(
                (p * ((coup[t, :, l] - alpha[...]) - shift[t, :, l]) * (1.0 / TEMPER)).astype(
                    jnp.bfloat16
                )
            )
            pb.append(p.astype(jnp.bfloat16))
        ds = jnp.concatenate(ds, axis=1)
        pb = jnp.concatenate(pb, axis=1)
        dqacc[...] += jnp.dot(ds, phat[t], preferred_element_type=jnp.float32)
        dp_out[t] = jnp.dot(
            left_t[0], ds, preferred_element_type=jnp.float32
        ) + jnp.dot(left_t[1], pb, preferred_element_type=jnp.float32)
        return carry

    lax.fori_loop(0, tiles, fifth, 0)

    piece = queries // cols
    copies = []
    for o in range(1, cols):
        peer = lax.rem(c + o, cols)
        cp = push(
            dqacc.at[pl.ds(pl.multiple_of(peer * piece, 8), piece)],
            cbuf.at[o, pl.ds(0, piece)], dsend.at[o], drecv.at[o], (r, peer),
        )
        cp.start()
        copies.append(cp)
    for cp in copies:
        cp.wait()
    mine = dqacc[pl.ds(pl.multiple_of(c * piece, 8), piece), :]
    for o in range(1, cols):
        mine = mine + cbuf[o, 0:piece]
    dq_out[...] = mine


def run_main(rows, cols, qhat, scaled, phat, offset, wgt, left_t):
    queries, feats = qhat.shape
    tiles, width, _ = phat.shape
    f32 = jnp.float32
    vec = lambda *s: pltpu.VMEM(s, f32)
    sems_r = [pltpu.SemaphoreType.DMA((rows,))] * 2
    sems_c = [pltpu.SemaphoreType.DMA((cols,))] * 2
    return pl.pallas_call(
        functools.partial(main_kernel, rows, cols),
        out_shape=(
            jax.ShapeDtypeStruct((tiles, feats, width), f32),
            jax.ShapeDtypeStruct((queries // cols, feats), f32),
        ),
        in_specs=[pl.BlockSpec(memory_space=pltpu.VMEM)] * 6,
        out_specs=(pl.BlockSpec(memory_space=pltpu.VMEM),) * 2,
        scratch_shapes=[
            vec(tiles, queries, width), vec(tiles, queries, width),
            vec(queries, LANES), vec(queries, LANES), vec(queries, LANES), vec(queries, LANES),
            vec(cols, queries, LANES),
            vec(tiles, 2, width), vec(rows, 2, width), vec(tiles, 1, width),
            vec(tiles, 1, width), vec(rows, 1, width), vec(tiles, 1, width),
            vec(1, width), vec(queries, feats), vec(cols, queries, LANES),
        ]
        + sems_c + sems_r + sems_r + sems_c + sems_r + sems_r + sems_c,
        compiler_params=pltpu.CompilerParams(
            collective_id=0, has_side_effects=True, vmem_limit_bytes=56 * 1024 * 1024
        ),
        name="transport_sweeps",
    )(qhat, scaled, phat, offset, wgt, left_t)


def local(rows, cols, queries, prototypes, potential, weights, capacity, cotangent):
    qhat, qlen = unit_rows(queries)
    phat, plen = unit_rows(prototypes)
    wgt = weights.astype(jnp.float32)
    scaled = (cotangent.astype(jnp.float32) / wgt[:, None]).astype(jnp.bfloat16)
    slots, feats = phat.shape
    width, tiles = tiles_of(slots, rows)
    offset = jnp.log2(capacity.astype(jnp.float32)) - potential * (1.0 / (TEMPER * math.log(2.0)))
    dp, dq = run_main(
        rows, cols, qhat, scaled, phat.reshape(tiles, width, feats),
        offset.reshape(tiles, 1, width),
        jnp.broadcast_to(wgt[:, None], (wgt.shape[0], LANES))[:, :1],
        jnp.stack([qhat.T, scaled.T]),
    )
    piece = dq.shape[0]
    begin = lax.axis_index("cols") * piece
    grad_queries = unit_back(
        dq,
        lax.dynamic_slice_in_dim(qhat, begin, piece, 0),
        lax.dynamic_slice_in_dim(qlen, begin, piece, 0),
    )
    whole = lax.psum(dp, "rows")
    whole = whole.transpose(0, 2, 1).reshape(slots, feats)
    grad_protos = unit_back(whole, phat, plen)
    return (grad_queries, grad_protos)


def solution(mesh):
    rows, cols = mesh.shape["rows"], mesh.shape["cols"]
    in_specs = (P("rows", None), P("cols", None), P("cols"), P("rows"), P("cols"), P("rows", None))
    out_specs = (P(("rows", "cols"), None), P("cols", None))
    return jax.shard_map(
        functools.partial(local, rows, cols),
        mesh=mesh, in_specs=in_specs, out_specs=out_specs, check_vma=False,
    )
```

```python
import functools
import math

import jax
import jax.numpy as jnp
from jax import lax
from jax.experimental import pallas as pl
from jax.experimental.pallas import tpu as pltpu
from jax.sharding import PartitionSpec as P

TEMPER = 0.05
LANES = 128
MESH = pl.DeviceIdType.MESH


def unit_rows(matrix):
    wide = matrix.astype(jnp.float32)
    length = jnp.sqrt(jnp.sum(wide * wide, axis=1) + 1e-06)
    return ((wide / length[:, None]).astype(jnp.bfloat16), length)


def unit_back(grad, unit, length):
    wide = unit.astype(jnp.float32)
    along = jnp.sum(wide * grad, axis=1, keepdims=True)
    return (grad - wide * along) / length[:, None]


def nt_dot(left, right):
    return lax.dot_general(
        left, right, (((1,), (1,)), ((), ())), preferred_element_type=jnp.float32
    )


def tiles_of(slots, rows):
    width = max(slots // rows, LANES)
    return width, slots // width


def push(src, dst, send, recv, device):
    return pltpu.make_async_remote_copy(
        src_ref=src, dst_ref=dst, send_sem=send, recv_sem=recv,
        device_id=device, device_id_type=MESH,
    )


def main_kernel(
    rows, cols, fused, qhat, scaled, phat, offset, wgt, left_t, plen, dp_out, dq_out,
    kern, coup, zacc, kacc, share, alpha, cbuf, part, pbuf, beta, gpart, gbuf, shift,
    invs, dqacc, dqbuf,
    csend, crecv, psend, precv, bsend, brecv, rsend, rrecv, gsend, grecv, hsend, hrecv,
    dsend, drecv, *ring,
):
    tiles, queries, width = kern.shape
    lanes = [slice(k, k + LANES) for k in range(0, width, LANES)]
    r = lax.axis_index("rows")
    c = lax.axis_index("cols")

    barrier = pltpu.get_barrier_semaphore()
    for o in range(1, rows):
        pl.semaphore_signal(
            barrier, inc=1, device_id=(lax.rem(r + o, rows), c), device_id_type=MESH
        )
    for o in range(1, cols):
        pl.semaphore_signal(
            barrier, inc=1, device_id=(r, lax.rem(c + o, cols)), device_id_type=MESH
        )

    zacc[...] = jnp.zeros_like(zacc)
    kacc[...] = jnp.zeros_like(kacc)
    dqacc[...] = jnp.zeros_like(dqacc)
    log2e = 1.0 / (TEMPER * math.log(2.0))
    step = min(queries, 256)

    def first(t, carry):
        proto = phat[t]
        base = offset[t]
        for q in range(0, queries, step):
            qs = slice(q, q + step)
            k = jnp.exp2(nt_dot(qhat[qs], proto) * log2e + base)
            g = nt_dot(scaled[qs], proto)
            kern[t, qs, :] = k
            coup[t, qs, :] = g
            kg = k * g
            zsum = k[:, lanes[0]]
            gsum = kg[:, lanes[0]]
            for l in lanes[1:]:
                zsum = zsum + k[:, l]
                gsum = gsum + kg[:, l]
            zacc[qs, :] += zsum
            kacc[qs, :] += gsum
        return carry

    lax.fori_loop(0, tiles, first, 0)
    pl.semaphore_wait(barrier, rows - 1 + cols - 1)

    lane = lax.broadcasted_iota(jnp.int32, (queries, LANES), 1)

    def over_cols(send, recv):
        copies = []
        for o in range(1, cols):
            cp = push(
                cbuf.at[0], cbuf.at[o], send.at[o], recv.at[o],
                (r, lax.rem(c + o, cols)),
            )
            cp.start()
            copies.append(cp)
        for cp in copies:
            cp.wait()
        total = cbuf[0]
        for o in range(1, cols):
            total = total + cbuf[o]
        return total

    ztot = jnp.sum(zacc[...], axis=1, keepdims=True)
    kgsum = jnp.sum(kacc[...], axis=1, keepdims=True)
    cbuf[0] = jnp.where(lane == 0, ztot, kgsum)
    total = over_cols(csend, crecv)
    ztot = total[:, 0:1]
    kgsum = total[:, 1:2]
    w = wgt[...]
    srate = w / ztot
    share[...] = jnp.broadcast_to(srate, share.shape)
    alpha[...] = jnp.broadcast_to(srate * kgsum / w, alpha.shape)

    def second(t, carry):
        for l in lanes:
            p = share[...] * kern[t, :, l]
            kern[t, :, l] = p
            part[t, 0:1, l] = jnp.sum(p, axis=0, keepdims=True)
            part[t, 1:2, l] = jnp.sum(
                p * (coup[t, :, l] - alpha[...]), axis=0, keepdims=True
            )
        return carry

    lax.fori_loop(0, tiles, second, 0)

    def scatter(src, dst, send, recv):
        def each(o, carry):
            peer = lax.rem(r + o, rows)

            def go():
                push(src.at[peer], dst.at[o], send.at[o], recv.at[o], (peer, c)).start()

            if tiles == rows:
                go()
            else:
                pl.when(peer < tiles)(go)
            return carry

        lax.fori_loop(1, rows, each, 0)

        def done(o, carry):
            peer = lax.rem(r + o, rows)

            def sent():
                push(src.at[0], dst.at[o], send.at[o], recv.at[o], (peer, c)).wait_send()

            def got():
                push(src.at[0], dst.at[o], send.at[o], recv.at[o], (peer, c)).wait_recv()

            if tiles == rows:
                sent()
                got()
            else:
                pl.when(peer < tiles)(sent)
                pl.when(r < tiles)(got)
            return carry

        lax.fori_loop(1, rows, done, 0)

    def spread(buf, send, recv):
        def each(o, carry):
            peer = lax.rem(r + o, rows)

            def go():
                push(buf.at[r], buf.at[r], send.at[o], recv.at[o], (peer, c)).start()

            if tiles == rows:
                go()
            else:
                pl.when(r < tiles)(go)
            return carry

        lax.fori_loop(1, rows, each, 0)

        def done(o, carry):
            origin = lax.rem(r + rows - o, rows)
            peer = lax.rem(r + o, rows)

            def sent():
                push(buf.at[r], buf.at[r], send.at[o], recv.at[o], (peer, c)).wait_send()

            def got():
                push(
                    buf.at[origin], buf.at[origin], send.at[o], recv.at[o], (peer, c)
                ).wait_recv()

            if tiles == rows:
                sent()
                got()
            else:
                pl.when(r < tiles)(sent)
                pl.when(origin < tiles)(got)
            return carry

        lax.fori_loop(1, rows, done, 0)

    def own(body):
        if tiles == rows:
            body()
        else:
            pl.when(r < tiles)(body)

    scatter(part, pbuf, psend, precv)

    def first_beta():
        both = part[r]
        for o in range(1, rows):
            both = both + pbuf[o]
        inv = 1.0 / both[0:1]
        invs[...] = inv
        beta[r] = both[1:2] * inv

    own(first_beta)
    spread(beta, bsend, brecv)

    zacc[...] = jnp.zeros_like(zacc)

    def third(t, carry):
        acc = zacc[...]
        for l in lanes:
            acc = acc + kern[t, :, l] * beta[t, :, l]
        zacc[...] = acc
        return carry

    lax.fori_loop(0, tiles, third, 0)
    rowprod = jnp.sum(zacc[...], axis=1, keepdims=True)
    cbuf2 = jnp.broadcast_to(rowprod, (queries, LANES))
    kacc[...] = cbuf2
    copies = []
    for o in range(1, cols):
        cp = push(
            kacc, dqbuf.at[o], rsend.at[o], rrecv.at[o], (r, lax.rem(c + o, cols))
        )
        cp.start()
        copies.append(cp)
    for cp in copies:
        cp.wait()
    rowtot = kacc[...]
    for o in range(1, cols):
        rowtot = rowtot + dqbuf[o]
    change = rowtot / w
    share[...] = change
    alpha[...] = alpha[...] - change

    def fourth(t, carry):
        for l in lanes:
            gpart[t, :, l] = jnp.sum(share[...] * kern[t, :, l], axis=0, keepdims=True)
        return carry

    lax.fori_loop(0, tiles, fourth, 0)
    scatter(gpart, gbuf, gsend, grecv)

    def second_beta():
        tot = gpart[r]
        for o in range(1, rows):
            tot = tot + gbuf[o]
        shift[r] = beta[r] + tot * invs[...]

    own(second_beta)
    spread(shift, hsend, hrecv)

    if fused:
        dp, rs1, rs2, rs3, s1s, s1r, s2s, s2r, s3s, s3r, as_, ar, bs, br, zs, zr = ring
    else:
        dp = dp_out

    def fifth(t):
        ds = []
        pb = []
        for l in lanes:
            p = kern[t, :, l]
            ds.append(
                (p * ((coup[t, :, l] - alpha[...]) - shift[t, :, l]) * (1.0 / TEMPER)).astype(
                    jnp.bfloat16
                )
            )
            pb.append(p.astype(jnp.bfloat16))
        ds = jnp.concatenate(ds, axis=1)
        pb = jnp.concatenate(pb, axis=1)
        dqacc[...] += jnp.dot(ds, phat[t], preferred_element_type=jnp.float32)
        dp[t] = jnp.dot(
            left_t[0], ds, preferred_element_type=jnp.float32
        ) + jnp.dot(left_t[1], pb, preferred_element_type=jnp.float32)

    if not fused:

        def plain(t, carry):
            fifth(t)
            return carry

        lax.fori_loop(0, tiles, plain, 0)
    else:
        depth = rows // 4
        z = r // 4
        even = lax.rem(c, 2) == 0
        wa = jnp.where(even, 1, 2)
        wb = 3 - wa
        a = jnp.where(even, lax.rem(r, 2), lax.rem(r // 2, 2))
        b = jnp.where(even, lax.rem(r // 2, 2), lax.rem(r, 2))
        peer_a = r + (1 - 2 * a) * wa
        peer_b = r + (1 - 2 * b) * wb

        def spot(zz, av, bv):
            return zz * 4 + av * wa + bv * wb

        def ahead(k):
            return lax.rem(z + 1 + k, depth)

        def copy_a1(i, t):
            return push(dp.at[t], rs1.at[i], s1s.at[i], s1r.at[i], (peer_a, c))

        def copy_b1(k, t):
            return push(dp.at[t], rs2.at[k], s2s.at[k], s2r.at[k], (peer_b, c))

        def copy_z1(k, t):
            return push(dp.at[t], rs3.at[k], s3s.at[k], s3r.at[k], (spot(ahead(k), a, b), c))

        def leave(i, carry):
            far = i < depth
            t = spot(ahead(lax.rem(i, depth)), 1 - a, jnp.where(far, 1 - b, b))
            fifth(t)
            copy_a1(i, t).start()
            return carry

        lax.fori_loop(0, 2 * depth, leave, 0)

        def stay(i, carry):
            far = i < depth
            fifth(spot(ahead(lax.rem(i, depth)), a, jnp.where(far, 1 - b, b)))
            return carry

        lax.fori_loop(0, 2 * depth, stay, 0)

    piece = queries // cols
    copies = []
    for o in range(1, cols):
        peer = lax.rem(c + o, cols)
        cp = push(
            dqacc.at[pl.ds(pl.multiple_of(peer * piece, 8), piece)],
            cbuf.at[o, pl.ds(0, piece)], dsend.at[o], drecv.at[o], (r, peer),
        )
        cp.start()
        copies.append(cp)

    if fused:

        def hop_b(k, carry):
            t = spot(ahead(k), a, 1 - b)
            copy_a1(k, t).wait_recv()
            dp[t] += rs1[k]
            copy_b1(k, t).start()
            return carry

        lax.fori_loop(0, depth, hop_b, 0)

        def hop_z(k, carry):
            t = spot(ahead(k), a, b)
            copy_a1(depth + k, t).wait_recv()
            copy_b1(k, t).wait_recv()
            dp[t] += rs1[depth + k] + rs2[k]
            if depth > 1:

                @pl.when(k < depth - 1)
                def _():
                    copy_z1(k, t).start()

            return carry

        lax.fori_loop(0, depth, hop_z, 0)
        total = dp[r]
        for k in range(depth - 1):
            copy_z1(k, r).wait_recv()
            total = total + rs3[k]
        unit = phat[r].astype(jnp.float32).T
        along = jnp.sum(unit * total, axis=0, keepdims=True)
        dp_out[r] = ((total - unit * along) / plen[r]).T

        def copy_a2(i, t):
            return push(dp_out.at[t], dp_out.at[t], as_.at[i], ar.at[i], (peer_a, c))

        def copy_b2(m, t):
            return push(dp_out.at[t], dp_out.at[t], bs.at[m], br.at[m], (peer_b, c))

        def copy_z2(k, t):
            return push(
                dp_out.at[t], dp_out.at[t], zs.at[k], zr.at[k], (spot(ahead(k), a, b), c)
            )

        def behind(m):
            return lax.rem(z + depth - m, depth)

        copy_a2(0, r).start()
        copy_b2(0, r).start()
        for k in range(depth - 1):
            copy_z2(k, r).start()
        for m in range(depth):
            if m > 0:
                t = spot(behind(m), a, b)
                copy_z2(m - 1, t).wait_recv()
                copy_b2(m, t).start()
                copy_a2(2 * m, t).start()
            t = spot(behind(m), a, 1 - b)
            copy_b2(m, t).wait_recv()
            copy_a2(2 * m + 1, t).start()
        for m in range(depth):
            copy_a2(2 * m, spot(behind(m), 1 - a, b)).wait_recv()
            copy_a2(2 * m + 1, spot(behind(m), 1 - a, 1 - b)).wait_recv()
        for k in range(2 * depth):
            copy_a1(k, r).wait_send()
            copy_a2(k, r).wait_send()
        for k in range(depth):
            copy_b1(k, r).wait_send()
            copy_b2(k, r).wait_send()
        for k in range(depth - 1):
            copy_z1(k, r).wait_send()
            copy_z2(k, r).wait_send()

    for cp in copies:
        cp.wait()
    mine = dqacc[pl.ds(pl.multiple_of(c * piece, 8), piece), :]
    for o in range(1, cols):
        mine = mine + cbuf[o, 0:piece]
    dq_out[...] = mine


def run_main(rows, cols, fused, qhat, scaled, phat, offset, wgt, left_t, plen):
    queries, feats = qhat.shape
    tiles, width, _ = phat.shape
    f32 = jnp.float32
    vec = lambda *s: pltpu.VMEM(s, f32)
    sems_r = [pltpu.SemaphoreType.DMA((rows,))] * 2
    sems_c = [pltpu.SemaphoreType.DMA((cols,))] * 2
    ring = []
    if fused:
        depth = rows // 4
        ring = [
            vec(tiles, feats, width), vec(2 * depth, feats, width),
            vec(depth, feats, width), vec(depth, feats, width),
        ]
        for count in (2, 1, 1, 2, 1, 1):
            ring += [pltpu.SemaphoreType.DMA((count * depth,))] * 2
    return pl.pallas_call(
        functools.partial(main_kernel, rows, cols, fused),
        out_shape=(
            jax.ShapeDtypeStruct((tiles, width, feats) if fused else (tiles, feats, width), f32),
            jax.ShapeDtypeStruct((queries // cols, feats), f32),
        ),
        in_specs=[pl.BlockSpec(memory_space=pltpu.VMEM)] * 7,
        out_specs=(pl.BlockSpec(memory_space=pltpu.VMEM),) * 2,
        scratch_shapes=[
            vec(tiles, queries, width), vec(tiles, queries, width),
            vec(queries, LANES), vec(queries, LANES), vec(queries, LANES), vec(queries, LANES),
            vec(cols, queries, LANES),
            vec(tiles, 2, width), vec(rows, 2, width), vec(tiles, 1, width),
            vec(tiles, 1, width), vec(rows, 1, width), vec(tiles, 1, width),
            vec(1, width), vec(queries, feats), vec(cols, queries, LANES),
        ]
        + sems_c + sems_r + sems_r + sems_c + sems_r + sems_r + sems_c + ring,
        compiler_params=pltpu.CompilerParams(
            collective_id=0, has_side_effects=True, vmem_limit_bytes=56 * 1024 * 1024
        ),
        name="transport_sweeps",
    )(qhat, scaled, phat, offset, wgt, left_t, plen)


def local(rows, cols, queries, prototypes, potential, weights, capacity, cotangent):
    qhat, qlen = unit_rows(queries)
    phat, plen = unit_rows(prototypes)
    wgt = weights.astype(jnp.float32)
    scaled = (cotangent.astype(jnp.float32) / wgt[:, None]).astype(jnp.bfloat16)
    slots, feats = phat.shape
    width, tiles = tiles_of(slots, rows)
    offset = jnp.log2(capacity.astype(jnp.float32)) - potential * (1.0 / (TEMPER * math.log(2.0)))
    fused = tiles == rows and rows % 4 == 0
    dp, dq = run_main(
        rows, cols, fused, qhat, scaled, phat.reshape(tiles, width, feats),
        offset.reshape(tiles, 1, width),
        jnp.broadcast_to(wgt[:, None], (wgt.shape[0], LANES))[:, :1],
        jnp.stack([qhat.T, scaled.T]),
        plen.reshape(tiles, 1, width),
    )
    piece = dq.shape[0]
    begin = lax.axis_index("cols") * piece
    grad_queries = unit_back(
        dq,
        lax.dynamic_slice_in_dim(qhat, begin, piece, 0),
        lax.dynamic_slice_in_dim(qlen, begin, piece, 0),
    )
    if fused:
        return (grad_queries, dp.reshape(slots, feats))
    whole = lax.psum(dp, "rows")
    whole = whole.transpose(0, 2, 1).reshape(slots, feats)
    grad_protos = unit_back(whole, phat, plen)
    return (grad_queries, grad_protos)


def solution(mesh):
    rows, cols = mesh.shape["rows"], mesh.shape["cols"]
    in_specs = (P("rows", None), P("cols", None), P("cols"), P("rows"), P("cols"), P("rows", None))
    out_specs = (P(("rows", "cols"), None), P("cols", None))
    return jax.shard_map(
        functools.partial(local, rows, cols),
        mesh=mesh, in_specs=in_specs, out_specs=out_specs, check_vma=False,
    )
```

```python
import functools
import math

import jax
import jax.numpy as jnp
from jax import lax
from jax.experimental import pallas as pl
from jax.experimental.pallas import tpu as pltpu
from jax.sharding import PartitionSpec as P

TEMPER = 0.05
LANES = 128
MESH = pl.DeviceIdType.MESH


def unit_rows(matrix):
    wide = matrix.astype(jnp.float32)
    length = jnp.sqrt(jnp.sum(wide * wide, axis=1, keepdims=True) + 1e-06)
    return ((wide / length).astype(jnp.bfloat16), length)


def unit_back(grad, unit, length):
    wide = unit.astype(jnp.float32)
    along = jnp.sum(wide * grad, axis=1, keepdims=True)
    return (grad - wide * along) / length


def nt_dot(left, right):
    return lax.dot_general(
        left, right, (((1,), (1,)), ((), ())), preferred_element_type=jnp.float32
    )


def tiles_of(slots, rows):
    width = max(slots // rows, LANES)
    return width, slots // width


def push(src, dst, send, recv, device):
    return pltpu.make_async_remote_copy(
        src_ref=src, dst_ref=dst, send_sem=send, recv_sem=recv,
        device_id=device, device_id_type=MESH,
    )


def main_kernel(
    rows, cols, fused, queries_in, protos_in, potential, weights, capacity, cotangent,
    dp_out, dq_out, qhat, scaled, phat, offset, wgt, left_t,
    kern, coup, zacc, kacc, share, alpha, cbuf, part, pbuf, beta, gpart, gbuf, shift,
    invs, dqacc, dqbuf,
    csend, crecv, psend, precv, bsend, brecv, rsend, rrecv, gsend, grecv, hsend, hrecv,
    dsend, drecv, *ring,
):
    tiles, queries, width = kern.shape
    lanes = [slice(k, k + LANES) for k in range(0, width, LANES)]
    r = lax.axis_index("rows")
    c = lax.axis_index("cols")

    barrier = pltpu.get_barrier_semaphore()
    for o in range(1, rows):
        pl.semaphore_signal(
            barrier, inc=1, device_id=(lax.rem(r + o, rows), c), device_id_type=MESH
        )
    for o in range(1, cols):
        pl.semaphore_signal(
            barrier, inc=1, device_id=(r, lax.rem(c + o, cols)), device_id_type=MESH
        )

    zacc[...] = jnp.zeros_like(zacc)
    kacc[...] = jnp.zeros_like(kacc)
    dqacc[...] = jnp.zeros_like(dqacc)
    log2e = 1.0 / (TEMPER * math.log(2.0))
    step = min(queries, 256)
    offset[...] = jnp.log2(capacity[...].astype(jnp.float32)) - potential[...] * log2e
    feats = qhat.shape[1]
    wgt[...] = jnp.broadcast_to(weights[...].astype(jnp.float32), (feats, queries)).T
    unit, _ = unit_rows(queries_in[...])
    qhat[...] = unit
    left_t[0] = unit.astype(jnp.float32).T.astype(jnp.bfloat16)
    unit = (cotangent[...].astype(jnp.float32) / wgt[...]).astype(jnp.bfloat16)
    scaled[...] = unit
    left_t[1] = unit.astype(jnp.float32).T.astype(jnp.bfloat16)

    def first(t, carry):
        proto, _ = unit_rows(protos_in[t])
        phat[t] = proto
        base = offset[t]
        for q in range(0, queries, step):
            qs = slice(q, q + step)
            k = jnp.exp2(nt_dot(qhat[qs], proto) * log2e + base)
            g = nt_dot(scaled[qs], proto)
            kern[t, qs, :] = k
            coup[t, qs, :] = g
            kg = k * g
            zsum = k[:, lanes[0]]
            gsum = kg[:, lanes[0]]
            for l in lanes[1:]:
                zsum = zsum + k[:, l]
                gsum = gsum + kg[:, l]
            zacc[qs, :] += zsum
            kacc[qs, :] += gsum
        return carry

    lax.fori_loop(0, tiles, first, 0)
    pl.semaphore_wait(barrier, rows - 1 + cols - 1)

    lane = lax.broadcasted_iota(jnp.int32, (queries, LANES), 1)

    def over_cols(send, recv):
        copies = []
        for o in range(1, cols):
            cp = push(
                cbuf.at[0], cbuf.at[o], send.at[o], recv.at[o],
                (r, lax.rem(c + o, cols)),
            )
            cp.start()
            copies.append(cp)
        for cp in copies:
            cp.wait()
        total = cbuf[0]
        for o in range(1, cols):
            total = total + cbuf[o]
        return total

    ztot = jnp.sum(zacc[...], axis=1, keepdims=True)
    kgsum = jnp.sum(kacc[...], axis=1, keepdims=True)
    cbuf[0] = jnp.where(lane == 0, ztot, kgsum)
    total = over_cols(csend, crecv)
    ztot = total[:, 0:1]
    kgsum = total[:, 1:2]
    w = wgt[:, 0:1]
    srate = w / ztot
    share[...] = jnp.broadcast_to(srate, share.shape)
    alpha[...] = jnp.broadcast_to(srate * kgsum / w, alpha.shape)

    def second(t, carry):
        for l in lanes:
            p = share[...] * kern[t, :, l]
            kern[t, :, l] = p
            part[t, 0:1, l] = jnp.sum(p, axis=0, keepdims=True)
            part[t, 1:2, l] = jnp.sum(
                p * (coup[t, :, l] - alpha[...]), axis=0, keepdims=True
            )
        return carry

    lax.fori_loop(0, tiles, second, 0)

    def scatter(src, dst, send, recv):
        def each(o, carry):
            peer = lax.rem(r + o, rows)

            def go():
                push(src.at[peer], dst.at[o], send.at[o], recv.at[o], (peer, c)).start()

            if tiles == rows:
                go()
            else:
                pl.when(peer < tiles)(go)
            return carry

        lax.fori_loop(1, rows, each, 0)

        def done(o, carry):
            peer = lax.rem(r + o, rows)

            def sent():
                push(src.at[0], dst.at[o], send.at[o], recv.at[o], (peer, c)).wait_send()

            def got():
                push(src.at[0], dst.at[o], send.at[o], recv.at[o], (peer, c)).wait_recv()

            if tiles == rows:
                sent()
                got()
            else:
                pl.when(peer < tiles)(sent)
                pl.when(r < tiles)(got)
            return carry

        lax.fori_loop(1, rows, done, 0)

    def spread(buf, send, recv):
        def each(o, carry):
            peer = lax.rem(r + o, rows)

            def go():
                push(buf.at[r], buf.at[r], send.at[o], recv.at[o], (peer, c)).start()

            if tiles == rows:
                go()
            else:
                pl.when(r < tiles)(go)
            return carry

        lax.fori_loop(1, rows, each, 0)

        def done(o, carry):
            origin = lax.rem(r + rows - o, rows)
            peer = lax.rem(r + o, rows)

            def sent():
                push(buf.at[r], buf.at[r], send.at[o], recv.at[o], (peer, c)).wait_send()

            def got():
                push(
                    buf.at[origin], buf.at[origin], send.at[o], recv.at[o], (peer, c)
                ).wait_recv()

            if tiles == rows:
                sent()
                got()
            else:
                pl.when(r < tiles)(sent)
                pl.when(origin < tiles)(got)
            return carry

        lax.fori_loop(1, rows, done, 0)

    def own(body):
        if tiles == rows:
            body()
        else:
            pl.when(r < tiles)(body)

    scatter(part, pbuf, psend, precv)

    def first_beta():
        both = part[r]
        for o in range(1, rows):
            both = both + pbuf[o]
        inv = 1.0 / both[0:1]
        invs[...] = inv
        beta[r] = both[1:2] * inv

    own(first_beta)
    spread(beta, bsend, brecv)

    zacc[...] = jnp.zeros_like(zacc)

    def third(t, carry):
        acc = zacc[...]
        for l in lanes:
            acc = acc + kern[t, :, l] * beta[t, :, l]
        zacc[...] = acc
        return carry

    lax.fori_loop(0, tiles, third, 0)
    rowprod = jnp.sum(zacc[...], axis=1, keepdims=True)
    cbuf2 = jnp.broadcast_to(rowprod, (queries, LANES))
    kacc[...] = cbuf2
    copies = []
    for o in range(1, cols):
        cp = push(
            kacc, dqbuf.at[o], rsend.at[o], rrecv.at[o], (r, lax.rem(c + o, cols))
        )
        cp.start()
        copies.append(cp)
    for cp in copies:
        cp.wait()
    rowtot = kacc[...]
    for o in range(1, cols):
        rowtot = rowtot + dqbuf[o]
    change = rowtot / w
    share[...] = change
    alpha[...] = alpha[...] - change

    def fourth(t, carry):
        for l in lanes:
            gpart[t, :, l] = jnp.sum(share[...] * kern[t, :, l], axis=0, keepdims=True)
        return carry

    lax.fori_loop(0, tiles, fourth, 0)
    scatter(gpart, gbuf, gsend, grecv)

    def second_beta():
        tot = gpart[r]
        for o in range(1, rows):
            tot = tot + gbuf[o]
        shift[r] = beta[r] + tot * invs[...]

    own(second_beta)
    spread(shift, hsend, hrecv)

    if fused:
        dp, rs1, rs2, rs3, s1s, s1r, s2s, s2r, s3s, s3r, as_, ar, bs, br, zs, zr = ring
    else:
        dp = dp_out

    def fifth(t):
        ds = []
        pb = []
        for l in lanes:
            p = kern[t, :, l]
            ds.append(
                (p * ((coup[t, :, l] - alpha[...]) - shift[t, :, l]) * (1.0 / TEMPER)).astype(
                    jnp.bfloat16
                )
            )
            pb.append(p.astype(jnp.bfloat16))
        ds = jnp.concatenate(ds, axis=1)
        pb = jnp.concatenate(pb, axis=1)
        dqacc[...] += jnp.dot(ds, phat[t], preferred_element_type=jnp.float32)
        grad = jnp.dot(
            left_t[0], ds, preferred_element_type=jnp.float32
        ) + jnp.dot(left_t[1], pb, preferred_element_type=jnp.float32)
        if fused:
            for h, l in enumerate(lanes):
                dp[t, h] = grad[:, l]
        else:
            dp[t] = grad

    if not fused:

        def plain(t, carry):
            fifth(t)
            return carry

        lax.fori_loop(0, tiles, plain, 0)
    else:
        depth = rows // 4
        z = r // 4
        even = lax.rem(c, 2) == 0
        wa = jnp.where(even, 1, 2)
        wb = 3 - wa
        a = jnp.where(even, lax.rem(r, 2), lax.rem(r // 2, 2))
        b = jnp.where(even, lax.rem(r // 2, 2), lax.rem(r, 2))
        peer_a = r + (1 - 2 * a) * wa
        peer_b = r + (1 - 2 * b) * wb

        def spot(zz, av, bv):
            return zz * 4 + av * wa + bv * wb

        def ahead(k):
            return lax.rem(z + 1 + k, depth)

        def copy_a1(i, t, h):
            return push(dp.at[t, h], rs1.at[i, h], s1s.at[i, h], s1r.at[i, h], (peer_a, c))

        def copy_b1(k, t, h):
            return push(dp.at[t, h], rs2.at[k, h], s2s.at[k, h], s2r.at[k, h], (peer_b, c))

        def copy_z1(k, t, h):
            return push(
                dp.at[t, h], rs3.at[k, h], s3s.at[k, h], s3r.at[k, h],
                (spot(ahead(k), a, b), c),
            )

        def away(i):
            return spot(ahead(lax.rem(i, depth)), 1 - a, jnp.where(i < depth, 1 - b, b))

        def leave(i, carry):
            t = away(i)
            fifth(t)
            copy_a1(i, t, 0).start()
            return carry

        lax.fori_loop(0, 2 * depth, leave, 0)

        def leave_piece(h):
            def each(i, carry):
                copy_a1(i, away(i), h).start()
                return carry

            lax.fori_loop(0, 2 * depth, each, 0)

        leave_piece(1)

        def stay(i, carry):
            fifth(spot(ahead(lax.rem(i, depth)), a, jnp.where(i < depth, 1 - b, b)))
            return carry

        lax.fori_loop(0, 2 * depth, stay, 0)

    piece = queries // cols
    copies = []
    for o in range(1, cols):
        peer = lax.rem(c + o, cols)
        cp = push(
            dqacc.at[pl.ds(pl.multiple_of(peer * piece, 8), piece)],
            cbuf.at[o, pl.ds(0, piece)], dsend.at[o], drecv.at[o], (r, peer),
        )
        cp.start()
        copies.append(cp)

    if fused:
        count = len(lanes)

        def hop_b(h):
            def each(k, carry):
                t = spot(ahead(k), a, 1 - b)
                copy_a1(k, t, h).wait_recv()
                dp[t, h] += rs1[k, h]
                copy_b1(k, t, h).start()
                return carry

            lax.fori_loop(0, depth, each, 0)

        def hop_z(h):
            def each(k, carry):
                t = spot(ahead(k), a, b)
                copy_a1(depth + k, t, h).wait_recv()
                copy_b1(k, t, h).wait_recv()
                dp[t, h] += rs1[depth + k, h] + rs2[k, h]

                @pl.when(k < depth - 1)
                def _():
                    copy_z1(k, t, h).start()

                return carry

            lax.fori_loop(0, depth, each, 0)

        def block(t, h):
            return dp_out.at[t, pl.ds(h * LANES, LANES)]

        def copy_a2(i, t, h):
            return push(block(t, h), block(t, h), as_.at[i, h], ar.at[i, h], (peer_a, c))

        def copy_b2(m, t, h):
            return push(block(t, h), block(t, h), bs.at[m, h], br.at[m, h], (peer_b, c))

        def copy_z2(k, t, h):
            return push(
                block(t, h), block(t, h), zs.at[k, h], zr.at[k, h],
                (spot(ahead(k), a, b), c),
            )

        def behind(m):
            return lax.rem(z + depth - m, depth)

        def settle(h):
            total = dp[r, h]
            for k in range(depth - 1):
                copy_z1(k, r, h).wait_recv()
                total = total + rs3[k, h]
            rows_h = pl.ds(h * LANES, LANES)
            unit, length = unit_rows(protos_in[r, rows_h])
            dp_out[r, rows_h] = unit_back(total.T, unit, length)
            copy_a2(0, r, h).start()
            copy_b2(0, r, h).start()
            for k in range(depth - 1):
                copy_z2(k, r, h).start()

        def pass_z(h):
            t = spot(z, a, 1 - b)
            copy_b2(0, t, h).wait_recv()
            copy_a2(1, t, h).start()
            for m in range(1, depth):
                t = spot(behind(m), a, b)
                copy_z2(m - 1, t, h).wait_recv()
                copy_b2(m, t, h).start()
                copy_a2(2 * m, t, h).start()

        def pass_b(h):
            for m in range(1, depth):
                t = spot(behind(m), a, 1 - b)
                copy_b2(m, t, h).wait_recv()
                copy_a2(2 * m + 1, t, h).start()

        for s in range(count + 4):
            if 2 <= s + 2 < count:
                leave_piece(s + 2)
            for lag, stage in ((4, pass_b), (3, pass_z), (2, settle), (1, hop_z), (0, hop_b)):
                if 0 <= s - lag < count:
                    stage(s - lag)

        def finish(h):
            for m in range(depth):
                copy_a2(2 * m, spot(behind(m), 1 - a, b), h).wait_recv()
                copy_a2(2 * m + 1, spot(behind(m), 1 - a, 1 - b), h).wait_recv()
            for k in range(2 * depth):
                copy_a1(k, r, h).wait_send()
                copy_a2(k, r, h).wait_send()
            for k in range(depth):
                copy_b1(k, r, h).wait_send()
                copy_b2(k, r, h).wait_send()
            for k in range(depth - 1):
                copy_z1(k, r, h).wait_send()
                copy_z2(k, r, h).wait_send()

        for h in range(count):
            finish(h)

    for cp in copies:
        cp.wait()
    begin = pl.ds(pl.multiple_of(c * piece, 16), piece)
    mine = dqacc[begin, :]
    for o in range(1, cols):
        mine = mine + cbuf[o, 0:piece]
    unit, length = unit_rows(queries_in[begin, :])
    dq_out[...] = unit_back(mine, unit, length)


def run_main(rows, cols, fused, *args):
    queries, feats = args[0].shape
    tiles, width, _ = args[1].shape
    bf16 = jnp.bfloat16
    f32 = jnp.float32
    vec = lambda *s: pltpu.VMEM(s, f32)
    sems_r = [pltpu.SemaphoreType.DMA((rows,))] * 2
    sems_c = [pltpu.SemaphoreType.DMA((cols,))] * 2
    ring = []
    if fused:
        depth = rows // 4
        cuts = width // LANES
        ring = [vec(n, cuts, feats, LANES) for n in (tiles, 2 * depth, depth, depth)]
        for count in (2, 1, 1, 2, 1, 1):
            ring += [pltpu.SemaphoreType.DMA((count * depth, cuts))] * 2
    return pl.pallas_call(
        functools.partial(main_kernel, rows, cols, fused),
        out_shape=(
            jax.ShapeDtypeStruct((tiles, width, feats) if fused else (tiles, feats, width), f32),
            jax.ShapeDtypeStruct((queries // cols, feats), f32),
        ),
        in_specs=[pl.BlockSpec(memory_space=pltpu.VMEM)] * 6,
        out_specs=(pl.BlockSpec(memory_space=pltpu.VMEM),) * 2,
        scratch_shapes=[
            pltpu.VMEM((queries, feats), bf16), pltpu.VMEM((queries, feats), bf16),
            pltpu.VMEM((tiles, width, feats), bf16), vec(tiles, 1, width),
            vec(queries, LANES), pltpu.VMEM((2, feats, queries), bf16),
            vec(tiles, queries, width), vec(tiles, queries, width),
            vec(queries, LANES), vec(queries, LANES), vec(queries, LANES), vec(queries, LANES),
            vec(cols, queries, LANES),
            vec(tiles, 2, width), vec(rows, 2, width), vec(tiles, 1, width),
            vec(tiles, 1, width), vec(rows, 1, width), vec(tiles, 1, width),
            vec(1, width), vec(queries, feats), vec(cols, queries, LANES),
        ]
        + sems_c + sems_r + sems_r + sems_c + sems_r + sems_r + sems_c + ring,
        compiler_params=pltpu.CompilerParams(
            collective_id=0, has_side_effects=True, vmem_limit_bytes=56 * 1024 * 1024
        ),
        name="transport_sweeps",
    )(*args)


def local(rows, cols, queries, prototypes, potential, weights, capacity, cotangent):
    slots, feats = prototypes.shape
    width, tiles = tiles_of(slots, rows)
    fused = tiles == rows and rows % 4 == 0
    dp, dq = run_main(
        rows, cols, fused, queries, prototypes.reshape(tiles, width, feats),
        potential.reshape(tiles, 1, width), weights.reshape(1, -1),
        capacity.reshape(tiles, 1, width), cotangent,
    )
    if fused:
        return (dq, dp.reshape(slots, feats))
    whole = lax.psum(dp, "rows")
    whole = whole.transpose(0, 2, 1).reshape(slots, feats)
    return (dq, unit_back(whole, *unit_rows(prototypes)))


def solution(mesh):
    rows, cols = mesh.shape["rows"], mesh.shape["cols"]
    in_specs = (P("rows", None), P("cols", None), P("cols"), P("rows"), P("cols"), P("rows", None))
    out_specs = (P(("rows", "cols"), None), P("cols", None))
    return jax.shard_map(
        functools.partial(local, rows, cols),
        mesh=mesh, in_specs=in_specs, out_specs=out_specs, check_vma=False,
    )
```

```python
import functools
import math

import jax
import jax.numpy as jnp
from jax import lax
from jax.experimental import pallas as pl
from jax.experimental.pallas import tpu as pltpu
from jax.sharding import PartitionSpec as P

TEMPER = 0.05
LANES = 128
MESH = pl.DeviceIdType.MESH


def unit_rows(matrix):
    wide = matrix.astype(jnp.float32)
    length = jnp.sqrt(jnp.sum(wide * wide, axis=1, keepdims=True) + 1e-06)
    return ((wide / length).astype(jnp.bfloat16), length)


def unit_back(grad, unit, length):
    wide = unit.astype(jnp.float32)
    along = jnp.sum(wide * grad, axis=1, keepdims=True)
    return (grad - wide * along) / length


def nt_dot(left, right):
    return lax.dot_general(
        left, right, (((1,), (1,)), ((), ())), preferred_element_type=jnp.float32
    )


def tiles_of(slots, rows):
    width = max(slots // rows, LANES)
    return width, slots // width


def push(src, dst, send, recv, device):
    return pltpu.make_async_remote_copy(
        src_ref=src, dst_ref=dst, send_sem=send, recv_sem=recv,
        device_id=device, device_id_type=MESH,
    )


def main_kernel(
    rows, cols, fused, queries_in, protos_in, potential, weights, capacity, cotangent,
    dp_out, dq_out, qhat, scaled, phat, offset, wgt, left_t,
    kern, coup, zacc, kacc, share, alpha, cbuf, part, pbuf, beta, gpart, gbuf, shift,
    invs, dqacc, dqbuf, rbuf,
    csend, crecv, psend, precv, bsend, brecv, rsend, rrecv, gsend, grecv, hsend, hrecv,
    dsend, drecv, *ring,
):
    tiles, queries, width = kern.shape
    lanes = [slice(k, k + LANES) for k in range(0, width, LANES)]
    r = lax.axis_index("rows")
    c = lax.axis_index("cols")

    barrier = pltpu.get_barrier_semaphore()
    for o in range(1, rows):
        pl.semaphore_signal(
            barrier, inc=1, device_id=(lax.rem(r + o, rows), c), device_id_type=MESH
        )
    for o in range(1, cols):
        pl.semaphore_signal(
            barrier, inc=1, device_id=(r, lax.rem(c + o, cols)), device_id_type=MESH
        )

    zacc[...] = jnp.zeros_like(zacc)
    kacc[...] = jnp.zeros_like(kacc)
    dqacc[...] = jnp.zeros_like(dqacc)
    log2e = 1.0 / (TEMPER * math.log(2.0))
    step = min(queries, 256)
    offset[...] = jnp.log2(capacity[...].astype(jnp.float32)) - potential[...] * log2e
    feats = qhat.shape[1]
    wgt[...] = jnp.broadcast_to(weights[...].astype(jnp.float32), (feats, queries)).T
    unit, _ = unit_rows(queries_in[...])
    qhat[...] = unit
    left_t[0] = unit.astype(jnp.float32).T.astype(jnp.bfloat16)
    unit = (cotangent[...].astype(jnp.float32) / wgt[...]).astype(jnp.bfloat16)
    scaled[...] = unit
    left_t[1] = unit.astype(jnp.float32).T.astype(jnp.bfloat16)

    def first(t, carry):
        proto, _ = unit_rows(protos_in[t])
        phat[t] = proto
        base = offset[t]
        for q in range(0, queries, step):
            qs = slice(q, q + step)
            k = jnp.exp2(nt_dot(qhat[qs], proto) * log2e + base)
            g = nt_dot(scaled[qs], proto)
            kern[t, qs, :] = k
            coup[t, qs, :] = g
            kg = k * g
            zsum = k[:, lanes[0]]
            gsum = kg[:, lanes[0]]
            for l in lanes[1:]:
                zsum = zsum + k[:, l]
                gsum = gsum + kg[:, l]
            zacc[qs, :] += zsum
            kacc[qs, :] += gsum
        return carry

    lax.fori_loop(0, tiles, first, 0)
    pl.semaphore_wait(barrier, rows - 1 + cols - 1)

    def tall(row):
        return jnp.broadcast_to(row, (LANES, queries)).T

    def flat(acc):
        return jnp.sum(acc[...].T, axis=0, keepdims=True)

    def over_cols(buf, send, recv):
        copies = []
        for o in range(1, cols):
            cp = push(
                buf.at[0], buf.at[o], send.at[o], recv.at[o], (r, lax.rem(c + o, cols))
            )
            cp.start()
            copies.append(cp)
        for cp in copies:
            cp.wait()
        total = buf[0]
        for o in range(1, cols):
            total = total + buf[o]
        return total

    cbuf[0, 0:1] = flat(zacc)
    cbuf[0, 1:2] = flat(kacc)
    total = over_cols(cbuf, csend, crecv)
    w = weights[...].astype(jnp.float32)
    srate = w / total[0:1]
    share[...] = tall(srate)
    alpha[...] = tall(srate * total[1:2] / w)
    direct = tiles == rows

    def swept(body, part_ref, buf, send, recv):
        if not direct:
            lax.fori_loop(0, tiles, lambda t, k: body(t) or k, 0)
            scatter(part_ref, buf, send, recv)
            return

        def each(o, carry):
            t = lax.rem(r + o, rows)
            body(t)

            @pl.when(o < rows)
            def _():
                push(part_ref.at[t], buf.at[o], send.at[o], recv.at[o], (t, c)).start()

            return carry

        lax.fori_loop(1, rows + 1, each, 0)

        def done(o, carry):
            push(part_ref.at[r], buf.at[o], send.at[o], recv.at[o], (lax.rem(r + o, rows), c)).wait()
            return carry

        lax.fori_loop(1, rows, done, 0)

    def second(t):
        for l in lanes:
            p = share[...] * kern[t, :, l]
            kern[t, :, l] = p
            part[t, 0:1, l] = jnp.sum(p, axis=0, keepdims=True)
            part[t, 1:2, l] = jnp.sum(
                p * (coup[t, :, l] - alpha[...]), axis=0, keepdims=True
            )

    def scatter(src, dst, send, recv):
        def each(o, carry):
            peer = lax.rem(r + o, rows)

            def go():
                push(src.at[peer], dst.at[o], send.at[o], recv.at[o], (peer, c)).start()

            if tiles == rows:
                go()
            else:
                pl.when(peer < tiles)(go)
            return carry

        lax.fori_loop(1, rows, each, 0)

        def done(o, carry):
            peer = lax.rem(r + o, rows)

            def sent():
                push(src.at[0], dst.at[o], send.at[o], recv.at[o], (peer, c)).wait_send()

            def got():
                push(src.at[0], dst.at[o], send.at[o], recv.at[o], (peer, c)).wait_recv()

            if tiles == rows:
                sent()
                got()
            else:
                pl.when(peer < tiles)(sent)
                pl.when(r < tiles)(got)
            return carry

        lax.fori_loop(1, rows, done, 0)

    def spread_start(buf, send, recv):
        def each(o, carry):
            peer = lax.rem(r + o, rows)

            def go():
                push(buf.at[r], buf.at[r], send.at[o], recv.at[o], (peer, c)).start()

            if tiles == rows:
                go()
            else:
                pl.when(r < tiles)(go)
            return carry

        lax.fori_loop(1, rows, each, 0)

    def spread_got(buf, send, recv, t):
        o = lax.rem(r + rows - t, rows)

        @pl.when(o > 0)
        def _():
            push(buf.at[t], buf.at[t], send.at[o], recv.at[o], (t, c)).wait_recv()

    def spread_sent(buf, send, recv):
        def done(o, carry):
            push(
                buf.at[r], buf.at[r], send.at[o], recv.at[o], (lax.rem(r + o, rows), c)
            ).wait_send()
            return carry

        lax.fori_loop(1, rows, done, 0)

    def spread_wait(buf, send, recv):
        def done(o, carry):
            origin = lax.rem(r + rows - o, rows)
            peer = lax.rem(r + o, rows)

            def sent():
                push(buf.at[r], buf.at[r], send.at[o], recv.at[o], (peer, c)).wait_send()

            def got():
                push(
                    buf.at[origin], buf.at[origin], send.at[o], recv.at[o], (peer, c)
                ).wait_recv()

            if tiles == rows:
                sent()
                got()
            else:
                pl.when(r < tiles)(sent)
                pl.when(origin < tiles)(got)
            return carry

        lax.fori_loop(1, rows, done, 0)

    def own(body):
        if tiles == rows:
            body()
        else:
            pl.when(r < tiles)(body)

    swept(second, part, pbuf, psend, precv)

    def first_beta():
        both = part[r]
        for o in range(1, rows):
            both = both + pbuf[o]
        inv = 1.0 / both[0:1]
        invs[...] = inv
        beta[r] = both[1:2] * inv

    own(first_beta)
    zacc[...] = jnp.zeros_like(zacc)
    spread_start(beta, bsend, brecv)
    if not direct:
        spread_wait(beta, bsend, brecv)

    def third(o, carry):
        t = o
        if direct:
            t = lax.rem(r + rows - o, rows)
            spread_got(beta, bsend, brecv, t)
        acc = zacc[...]
        for l in lanes:
            acc = acc + kern[t, :, l] * beta[t, :, l]
        zacc[...] = acc
        return carry

    lax.fori_loop(0, tiles, third, 0)
    rbuf[0] = flat(zacc)
    change = tall(over_cols(rbuf, rsend, rrecv) / w)
    share[...] = change
    alpha[...] = alpha[...] - change

    def fourth(t):
        for l in lanes:
            gpart[t, :, l] = jnp.sum(share[...] * kern[t, :, l], axis=0, keepdims=True)

    swept(fourth, gpart, gbuf, gsend, grecv)

    def second_beta():
        tot = gpart[r]
        for o in range(1, rows):
            tot = tot + gbuf[o]
        shift[r] = beta[r] + tot * invs[...]

    own(second_beta)
    spread_start(shift, hsend, hrecv)
    if not direct:
        spread_wait(shift, hsend, hrecv)

    if fused:
        dp, rs1, rs2, rs3, s1s, s1r, s2s, s2r, s3s, s3r, as_, ar, bs, br, zs, zr = ring
    else:
        dp = dp_out

    def fifth(t):
        if direct:
            spread_got(shift, hsend, hrecv, t)
        ds = []
        pb = []
        for l in lanes:
            p = kern[t, :, l]
            ds.append(
                (p * ((coup[t, :, l] - alpha[...]) - shift[t, :, l]) * (1.0 / TEMPER)).astype(
                    jnp.bfloat16
                )
            )
            pb.append(p.astype(jnp.bfloat16))
        ds = jnp.concatenate(ds, axis=1)
        pb = jnp.concatenate(pb, axis=1)
        dqacc[...] += jnp.dot(ds, phat[t], preferred_element_type=jnp.float32)
        grad = jnp.dot(
            left_t[0], ds, preferred_element_type=jnp.float32
        ) + jnp.dot(left_t[1], pb, preferred_element_type=jnp.float32)
        if fused:
            for h, l in enumerate(lanes):
                dp[t, h] = grad[:, l]
        else:
            dp[t] = grad

    if not fused:

        def plain(t, carry):
            fifth(t)
            return carry

        lax.fori_loop(0, tiles, plain, 0)
    else:
        depth = rows // 4
        z = r // 4
        even = lax.rem(c, 2) == 0
        wa = jnp.where(even, 1, 2)
        wb = 3 - wa
        a = jnp.where(even, lax.rem(r, 2), lax.rem(r // 2, 2))
        b = jnp.where(even, lax.rem(r // 2, 2), lax.rem(r, 2))
        peer_a = r + (1 - 2 * a) * wa
        peer_b = r + (1 - 2 * b) * wb

        def spot(zz, av, bv):
            return zz * 4 + av * wa + bv * wb

        def ahead(k):
            return lax.rem(z + 1 + k, depth)

        def copy_a1(i, t, h):
            return push(dp.at[t, h], rs1.at[i, h], s1s.at[i, h], s1r.at[i, h], (peer_a, c))

        def copy_b1(k, t, h):
            return push(dp.at[t, h], rs2.at[k, h], s2s.at[k, h], s2r.at[k, h], (peer_b, c))

        def copy_z1(k, t, h):
            return push(
                dp.at[t, h], rs3.at[k, h], s3s.at[k, h], s3r.at[k, h],
                (spot(ahead(k), a, b), c),
            )

        def away(i):
            return spot(ahead(lax.rem(i, depth)), 1 - a, jnp.where(i < depth, 1 - b, b))

        def leave(i, carry):
            t = away(i)
            fifth(t)
            copy_a1(i, t, 0).start()
            return carry

        lax.fori_loop(0, 2 * depth, leave, 0)

        def leave_piece(h):
            def each(i, carry):
                copy_a1(i, away(i), h).start()
                return carry

            lax.fori_loop(0, 2 * depth, each, 0)

        leave_piece(1)

        def stay(i, carry):
            fifth(spot(ahead(lax.rem(i, depth)), a, jnp.where(i < depth, 1 - b, b)))
            return carry

        lax.fori_loop(0, 2 * depth, stay, 0)

    piece = queries // cols
    copies = []
    for o in range(1, cols):
        peer = lax.rem(c + o, cols)
        cp = push(
            dqacc.at[pl.ds(pl.multiple_of(peer * piece, 8), piece)],
            dqbuf.at[o], dsend.at[o], drecv.at[o], (r, peer),
        )
        cp.start()
        copies.append(cp)

    if fused:
        count = len(lanes)

        def hop_b(h):
            def each(k, carry):
                t = spot(ahead(k), a, 1 - b)
                copy_a1(k, t, h).wait_recv()
                dp[t, h] += rs1[k, h]
                copy_b1(k, t, h).start()
                return carry

            lax.fori_loop(0, depth, each, 0)

        def hop_z(h):
            def each(k, carry):
                t = spot(ahead(k), a, b)
                copy_a1(depth + k, t, h).wait_recv()
                copy_b1(k, t, h).wait_recv()
                dp[t, h] += rs1[depth + k, h] + rs2[k, h]

                @pl.when(k < depth - 1)
                def _():
                    copy_z1(k, t, h).start()

                return carry

            lax.fori_loop(0, depth, each, 0)

        def block(t, h):
            return dp_out.at[t, pl.ds(h * LANES, LANES)]

        def copy_a2(i, t, h):
            return push(block(t, h), block(t, h), as_.at[i, h], ar.at[i, h], (peer_a, c))

        def copy_b2(m, t, h):
            return push(block(t, h), block(t, h), bs.at[m, h], br.at[m, h], (peer_b, c))

        def copy_z2(k, t, h):
            return push(
                block(t, h), block(t, h), zs.at[k, h], zr.at[k, h],
                (spot(ahead(k), a, b), c),
            )

        def behind(m):
            return lax.rem(z + depth - m, depth)

        def settle(h):
            total = dp[r, h]
            for k in range(depth - 1):
                copy_z1(k, r, h).wait_recv()
                total = total + rs3[k, h]
            rows_h = pl.ds(h * LANES, LANES)
            unit, length = unit_rows(protos_in[r, rows_h])
            dp_out[r, rows_h] = unit_back(total.T, unit, length)
            copy_a2(0, r, h).start()
            copy_b2(0, r, h).start()
            for k in range(depth - 1):
                copy_z2(k, r, h).start()

        def pass_z(h):
            t = spot(z, a, 1 - b)
            copy_b2(0, t, h).wait_recv()
            copy_a2(1, t, h).start()
            for m in range(1, depth):
                t = spot(behind(m), a, b)
                copy_z2(m - 1, t, h).wait_recv()
                copy_b2(m, t, h).start()
                copy_a2(2 * m, t, h).start()

        def pass_b(h):
            for m in range(1, depth):
                t = spot(behind(m), a, 1 - b)
                copy_b2(m, t, h).wait_recv()
                copy_a2(2 * m + 1, t, h).start()

        for s in range(count + 4):
            if 2 <= s + 2 < count:
                leave_piece(s + 2)
            for lag, stage in ((4, pass_b), (3, pass_z), (2, settle), (1, hop_z), (0, hop_b)):
                if 0 <= s - lag < count:
                    stage(s - lag)

        def finish(h):
            for m in range(depth):
                copy_a2(2 * m, spot(behind(m), 1 - a, b), h).wait_recv()
                copy_a2(2 * m + 1, spot(behind(m), 1 - a, 1 - b), h).wait_recv()
            for k in range(2 * depth):
                copy_a1(k, r, h).wait_send()
                copy_a2(k, r, h).wait_send()
            for k in range(depth):
                copy_b1(k, r, h).wait_send()
                copy_b2(k, r, h).wait_send()
            for k in range(depth - 1):
                copy_z1(k, r, h).wait_send()
                copy_z2(k, r, h).wait_send()

        for h in range(count):
            finish(h)

    if direct:
        spread_sent(beta, bsend, brecv)
        spread_sent(shift, hsend, hrecv)
    for cp in copies:
        cp.wait()
    begin = pl.ds(pl.multiple_of(c * piece, 16), piece)
    mine = dqacc[begin, :]
    for o in range(1, cols):
        mine = mine + dqbuf[o]
    unit, length = unit_rows(queries_in[begin, :])
    dq_out[...] = unit_back(mine, unit, length)


def run_main(rows, cols, fused, *args):
    queries, feats = args[0].shape
    tiles, width, _ = args[1].shape
    bf16 = jnp.bfloat16
    f32 = jnp.float32
    vec = lambda *s: pltpu.VMEM(s, f32)
    sems_r = [pltpu.SemaphoreType.DMA((rows,))] * 2
    sems_c = [pltpu.SemaphoreType.DMA((cols,))] * 2
    ring = []
    if fused:
        depth = rows // 4
        cuts = width // LANES
        ring = [vec(n, cuts, feats, LANES) for n in (tiles, 2 * depth, depth, depth)]
        for count in (2, 1, 1, 2, 1, 1):
            ring += [pltpu.SemaphoreType.DMA((count * depth, cuts))] * 2
    return pl.pallas_call(
        functools.partial(main_kernel, rows, cols, fused),
        out_shape=(
            jax.ShapeDtypeStruct((tiles, width, feats) if fused else (tiles, feats, width), f32),
            jax.ShapeDtypeStruct((queries // cols, feats), f32),
        ),
        in_specs=[pl.BlockSpec(memory_space=pltpu.VMEM)] * 6,
        out_specs=(pl.BlockSpec(memory_space=pltpu.VMEM),) * 2,
        scratch_shapes=[
            pltpu.VMEM((queries, feats), bf16), pltpu.VMEM((queries, feats), bf16),
            pltpu.VMEM((tiles, width, feats), bf16), vec(tiles, 1, width),
            vec(queries, LANES), pltpu.VMEM((2, feats, queries), bf16),
            vec(tiles, queries, width), vec(tiles, queries, width),
            vec(queries, LANES), vec(queries, LANES), vec(queries, LANES), vec(queries, LANES),
            vec(cols, 2, queries),
            vec(tiles, 2, width), vec(rows, 2, width), vec(tiles, 1, width),
            vec(tiles, 1, width), vec(rows, 1, width), vec(tiles, 1, width),
            vec(1, width), vec(queries, feats),
            vec(cols, queries // cols, feats), vec(cols, 1, queries),
        ]
        + sems_c + sems_r + sems_r + sems_c + sems_r + sems_r + sems_c + ring,
        compiler_params=pltpu.CompilerParams(
            collective_id=0, has_side_effects=True, vmem_limit_bytes=56 * 1024 * 1024
        ),
        name="transport_sweeps",
    )(*args)


def hand_over(dp, dq, dp_out, dq_out, sems):
    step = dp.shape[0] // 8
    copies = [pltpu.make_async_copy(dq, dq_out, sems.at[8])]
    for k in range(8):
        part = pl.ds(k * step, step)
        copies.append(pltpu.make_async_copy(dp.at[part], dp_out.at[part], sems.at[k]))
    for cp in copies:
        cp.start()
    for cp in copies:
        cp.wait()


def run_hand_over(dp, dq):
    anywhere = pl.BlockSpec(memory_space=pl.ANY)
    return pl.pallas_call(
        hand_over,
        out_shape=(
            jax.ShapeDtypeStruct(dp.shape, dp.dtype), jax.ShapeDtypeStruct(dq.shape, dq.dtype)
        ),
        in_specs=[anywhere] * 2,
        out_specs=(anywhere,) * 2,
        scratch_shapes=[pltpu.SemaphoreType.DMA((9,))],
        name="hand_over",
    )(dp, dq)


def local(rows, cols, queries, prototypes, potential, weights, capacity, cotangent):
    slots, feats = prototypes.shape
    width, tiles = tiles_of(slots, rows)
    fused = tiles == rows and rows % 4 == 0
    dp, dq = run_main(
        rows, cols, fused, queries, prototypes.reshape(tiles, width, feats),
        potential.reshape(tiles, 1, width), weights.reshape(1, -1),
        capacity.reshape(tiles, 1, width), cotangent,
    )
    if fused:
        grad_protos, grad_queries = run_hand_over(dp.reshape(slots, feats), dq)
        return (grad_queries, grad_protos)
    whole = lax.psum(dp, "rows")
    whole = whole.transpose(0, 2, 1).reshape(slots, feats)
    return (dq, unit_back(whole, *unit_rows(prototypes)))


def solution(mesh):
    rows, cols = mesh.shape["rows"], mesh.shape["cols"]
    in_specs = (P("rows", None), P("cols", None), P("cols"), P("rows"), P("cols"), P("rows", None))
    out_specs = (P(("rows", "cols"), None), P("cols", None))
    return jax.shard_map(
        functools.partial(local, rows, cols),
        mesh=mesh, in_specs=in_specs, out_specs=out_specs, check_vma=False,
    )
```

```python
import functools
import math

import jax
import jax.numpy as jnp
from jax import lax
from jax.experimental import pallas as pl
from jax.experimental.pallas import tpu as pltpu
from jax.sharding import PartitionSpec as P

TEMPER = 0.05
LANES = 128
MESH = pl.DeviceIdType.MESH


def unit_rows(matrix):
    wide = matrix.astype(jnp.float32)
    length = jnp.sqrt(jnp.sum(wide * wide, axis=1, keepdims=True) + 1e-06)
    return ((wide / length).astype(jnp.bfloat16), length)


def unit_back(grad, unit, length):
    wide = unit.astype(jnp.float32)
    along = jnp.sum(wide * grad, axis=1, keepdims=True)
    return (grad - wide * along) / length


def nt_dot(left, right):
    return lax.dot_general(
        left, right, (((1,), (1,)), ((), ())), preferred_element_type=jnp.float32
    )


def tiles_of(slots, rows):
    width = max(slots // rows, LANES)
    return width, slots // width


def push(src, dst, send, recv, device):
    return pltpu.make_async_remote_copy(
        src_ref=src, dst_ref=dst, send_sem=send, recv_sem=recv,
        device_id=device, device_id_type=MESH,
    )


def main_kernel(
    rows, cols, fused, queries_in, protos_in, potential, weights, capacity, cotangent,
    dp_out, dq_out, qhat, scaled, phat, offset, wgt, left_t,
    kern, coup, zacc, kacc, share, alpha, cbuf, part, pbuf, beta, gpart, gbuf, shift,
    invs, dqacc, dqbuf, rbuf,
    csend, crecv, psend, precv, bsend, brecv, rsend, rrecv, gsend, grecv, hsend, hrecv,
    dsend, drecv, *ring,
):
    tiles, queries, width = kern.shape
    lanes = [slice(k, k + LANES) for k in range(0, width, LANES)]
    r = lax.axis_index("rows")
    c = lax.axis_index("cols")

    barrier = pltpu.get_barrier_semaphore()
    for o in range(1, rows):
        pl.semaphore_signal(
            barrier, inc=1, device_id=(lax.rem(r + o, rows), c), device_id_type=MESH
        )
    for o in range(1, cols):
        pl.semaphore_signal(
            barrier, inc=1, device_id=(r, lax.rem(c + o, cols)), device_id_type=MESH
        )

    zacc[...] = jnp.zeros_like(zacc)
    kacc[...] = jnp.zeros_like(kacc)
    dqacc[...] = jnp.zeros_like(dqacc)
    log2e = 1.0 / (TEMPER * math.log(2.0))
    step = min(queries, 256)
    offset[...] = jnp.log2(capacity[...].astype(jnp.float32)) - potential[...] * log2e
    feats = qhat.shape[1]
    wgt[...] = jnp.broadcast_to(weights[...].astype(jnp.float32), (feats, queries)).T
    unit, _ = unit_rows(queries_in[...])
    qhat[...] = unit
    left_t[0] = unit.astype(jnp.float32).T.astype(jnp.bfloat16)
    unit = (cotangent[...].astype(jnp.float32) / wgt[...]).astype(jnp.bfloat16)
    scaled[...] = unit
    left_t[1] = unit.astype(jnp.float32).T.astype(jnp.bfloat16)

    def first(t, carry):
        proto, _ = unit_rows(protos_in[t])
        phat[t] = proto
        base = offset[t]
        for q in range(0, queries, step):
            qs = slice(q, q + step)
            k = jnp.exp2(nt_dot(qhat[qs], proto) * log2e + base)
            g = nt_dot(scaled[qs], proto)
            kern[t, qs, :] = k
            coup[t, qs, :] = g
            kg = k * g
            zsum = k[:, lanes[0]]
            gsum = kg[:, lanes[0]]
            for l in lanes[1:]:
                zsum = zsum + k[:, l]
                gsum = gsum + kg[:, l]
            zacc[qs, :] += zsum
            kacc[qs, :] += gsum
        return carry

    lax.fori_loop(0, tiles, first, 0)
    pl.semaphore_wait(barrier, rows - 1 + cols - 1)

    def tall(row):
        return jnp.broadcast_to(row, (LANES, queries)).T

    def flat(acc):
        return jnp.sum(acc[...].T, axis=0, keepdims=True)

    def over_cols(buf, send, recv):
        copies = []
        for o in range(1, cols):
            cp = push(
                buf.at[0], buf.at[o], send.at[o], recv.at[o], (r, lax.rem(c + o, cols))
            )
            cp.start()
            copies.append(cp)
        for cp in copies:
            cp.wait()
        total = buf[0]
        for o in range(1, cols):
            total = total + buf[o]
        return total

    cbuf[0, 0:1] = flat(zacc)
    cbuf[0, 1:2] = flat(kacc)
    total = over_cols(cbuf, csend, crecv)
    w = weights[...].astype(jnp.float32)
    srate = w / total[0:1]
    share[...] = tall(srate)
    alpha[...] = tall(srate * total[1:2] / w)
    direct = tiles == rows

    def swept(body, part_ref, buf, send, recv):
        if not direct:
            lax.fori_loop(0, tiles, lambda t, k: body(t) or k, 0)
            scatter(part_ref, buf, send, recv)
            return

        def each(o, carry):
            t = lax.rem(r + o, rows)
            body(t)

            @pl.when(o < rows)
            def _():
                push(part_ref.at[t], buf.at[o], send.at[o], recv.at[o], (t, c)).start()

            return carry

        lax.fori_loop(1, rows + 1, each, 0)

        def done(o, carry):
            push(part_ref.at[r], buf.at[o], send.at[o], recv.at[o], (lax.rem(r + o, rows), c)).wait()
            return carry

        lax.fori_loop(1, rows, done, 0)

    def second(t):
        for l in lanes:
            p = share[...] * kern[t, :, l]
            kern[t, :, l] = p
            part[t, 0:1, l] = jnp.sum(p, axis=0, keepdims=True)
            part[t, 1:2, l] = jnp.sum(
                p * (coup[t, :, l] - alpha[...]), axis=0, keepdims=True
            )

    def scatter(src, dst, send, recv):
        def each(o, carry):
            peer = lax.rem(r + o, rows)

            def go():
                push(src.at[peer], dst.at[o], send.at[o], recv.at[o], (peer, c)).start()

            if tiles == rows:
                go()
            else:
                pl.when(peer < tiles)(go)
            return carry

        lax.fori_loop(1, rows, each, 0)

        def done(o, carry):
            peer = lax.rem(r + o, rows)

            def sent():
                push(src.at[0], dst.at[o], send.at[o], recv.at[o], (peer, c)).wait_send()

            def got():
                push(src.at[0], dst.at[o], send.at[o], recv.at[o], (peer, c)).wait_recv()

            if tiles == rows:
                sent()
                got()
            else:
                pl.when(peer < tiles)(sent)
                pl.when(r < tiles)(got)
            return carry

        lax.fori_loop(1, rows, done, 0)

    def spread_start(buf, send, recv):
        def each(o, carry):
            peer = lax.rem(r + o, rows)

            def go():
                push(buf.at[r], buf.at[r], send.at[o], recv.at[o], (peer, c)).start()

            if tiles == rows:
                go()
            else:
                pl.when(r < tiles)(go)
            return carry

        lax.fori_loop(1, rows, each, 0)

    def spread_got(buf, send, recv, t):
        o = lax.rem(r + rows - t, rows)

        @pl.when(o > 0)
        def _():
            push(buf.at[t], buf.at[t], send.at[o], recv.at[o], (t, c)).wait_recv()

    def spread_sent(buf, send, recv):
        def done(o, carry):
            push(
                buf.at[r], buf.at[r], send.at[o], recv.at[o], (lax.rem(r + o, rows), c)
            ).wait_send()
            return carry

        lax.fori_loop(1, rows, done, 0)

    def spread_wait(buf, send, recv):
        def done(o, carry):
            origin = lax.rem(r + rows - o, rows)
            peer = lax.rem(r + o, rows)

            def sent():
                push(buf.at[r], buf.at[r], send.at[o], recv.at[o], (peer, c)).wait_send()

            def got():
                push(
                    buf.at[origin], buf.at[origin], send.at[o], recv.at[o], (peer, c)
                ).wait_recv()

            if tiles == rows:
                sent()
                got()
            else:
                pl.when(r < tiles)(sent)
                pl.when(origin < tiles)(got)
            return carry

        lax.fori_loop(1, rows, done, 0)

    def own(body):
        if tiles == rows:
            body()
        else:
            pl.when(r < tiles)(body)

    swept(second, part, pbuf, psend, precv)

    def first_beta():
        both = part[r]
        for o in range(1, rows):
            both = both + pbuf[o]
        inv = 1.0 / both[0:1]
        invs[...] = inv
        beta[r] = both[1:2] * inv

    own(first_beta)
    zacc[...] = jnp.zeros_like(zacc)
    spread_start(beta, bsend, brecv)
    if not direct:
        spread_wait(beta, bsend, brecv)

    def third(o, carry):
        t = o
        if direct:
            t = lax.rem(r + rows - o, rows)
            spread_got(beta, bsend, brecv, t)
        acc = zacc[...]
        for l in lanes:
            acc = acc + kern[t, :, l] * beta[t, :, l]
        zacc[...] = acc
        return carry

    lax.fori_loop(0, tiles, third, 0)
    rbuf[0] = flat(zacc)
    change = tall(over_cols(rbuf, rsend, rrecv) / w)
    share[...] = change
    alpha[...] = alpha[...] - change

    def fourth(t):
        for l in lanes:
            gpart[t, :, l] = jnp.sum(share[...] * kern[t, :, l], axis=0, keepdims=True)

    swept(fourth, gpart, gbuf, gsend, grecv)

    def second_beta():
        tot = gpart[r]
        for o in range(1, rows):
            tot = tot + gbuf[o]
        shift[r] = beta[r] + tot * invs[...]

    own(second_beta)
    spread_start(shift, hsend, hrecv)
    if not direct:
        spread_wait(shift, hsend, hrecv)

    if fused:
        dp, rs1, rs2, rs3, s1s, s1r, s2s, s2r, s3s, s3r, as_, ar, bs, br, zs, zr = ring
    else:
        dp = dp_out

    def fifth(t):
        if direct:
            spread_got(shift, hsend, hrecv, t)
        ds = []
        pb = []
        for l in lanes:
            p = kern[t, :, l]
            ds.append(
                (p * ((coup[t, :, l] - alpha[...]) - shift[t, :, l]) * (1.0 / TEMPER)).astype(
                    jnp.bfloat16
                )
            )
            pb.append(p.astype(jnp.bfloat16))
        ds = jnp.concatenate(ds, axis=1)
        pb = jnp.concatenate(pb, axis=1)
        dqacc[...] += jnp.dot(ds, phat[t], preferred_element_type=jnp.float32)
        grad = jnp.dot(
            left_t[0], ds, preferred_element_type=jnp.float32
        ) + jnp.dot(left_t[1], pb, preferred_element_type=jnp.float32)
        if fused:
            for h, l in enumerate(lanes):
                dp[t, h] = grad[:, l]
        else:
            dp[t] = grad

    if not fused:

        def plain(t, carry):
            fifth(t)
            return carry

        lax.fori_loop(0, tiles, plain, 0)
    else:
        depth = rows // 4
        z = r // 4
        even = lax.rem(c, 2) == 0
        wa = jnp.where(even, 1, 2)
        wb = 3 - wa
        a = jnp.where(even, lax.rem(r, 2), lax.rem(r // 2, 2))
        b = jnp.where(even, lax.rem(r // 2, 2), lax.rem(r, 2))
        peer_a = r + (1 - 2 * a) * wa
        peer_b = r + (1 - 2 * b) * wb

        def spot(zz, av, bv):
            return zz * 4 + av * wa + bv * wb

        def ahead(k):
            return lax.rem(z + 1 + k, depth)

        def copy_a1(i, t, h):
            return push(dp.at[t, h], rs1.at[i, h], s1s.at[i, h], s1r.at[i, h], (peer_a, c))

        def copy_b1(k, t, h):
            return push(dp.at[t, h], rs2.at[k, h], s2s.at[k, h], s2r.at[k, h], (peer_b, c))

        def copy_z1(k, t, h):
            return push(
                dp.at[t, h], rs3.at[k, h], s3s.at[k, h], s3r.at[k, h],
                (spot(ahead(k), a, b), c),
            )

        def away(i):
            return spot(ahead(lax.rem(i, depth)), 1 - a, jnp.where(i < depth, 1 - b, b))

        def leave(i, carry):
            t = away(i)
            fifth(t)
            copy_a1(i, t, 0).start()
            return carry

        lax.fori_loop(0, 2 * depth, leave, 0)

        def leave_piece(h):
            def each(i, carry):
                copy_a1(i, away(i), h).start()
                return carry

            lax.fori_loop(0, 2 * depth, each, 0)

        leave_piece(1)

        def stay(i, carry):
            fifth(spot(ahead(lax.rem(i, depth)), a, jnp.where(i < depth, 1 - b, b)))
            return carry

        lax.fori_loop(0, 2 * depth, stay, 0)

    piece = queries // cols
    copies = []
    for o in range(1, cols):
        peer = lax.rem(c + o, cols)
        cp = push(
            dqacc.at[pl.ds(pl.multiple_of(peer * piece, 8), piece)],
            dqbuf.at[o], dsend.at[o], drecv.at[o], (r, peer),
        )
        cp.start()
        copies.append(cp)

    def queries_done():
        for cp in copies:
            cp.wait()
        begin = pl.ds(pl.multiple_of(c * piece, 16), piece)
        mine = dqacc[begin, :]
        for o in range(1, cols):
            mine = mine + dqbuf[o]
        unit, length = unit_rows(queries_in[begin, :])
        dq_out[...] = unit_back(mine, unit, length)

    if fused:
        count = len(lanes)

        def hop_b(h):
            def each(k, carry):
                t = spot(ahead(k), a, 1 - b)
                copy_a1(k, t, h).wait_recv()
                dp[t, h] += rs1[k, h]
                copy_b1(k, t, h).start()
                return carry

            lax.fori_loop(0, depth, each, 0)

        def hop_z(h):
            def each(k, carry):
                t = spot(ahead(k), a, b)
                copy_a1(depth + k, t, h).wait_recv()
                copy_b1(k, t, h).wait_recv()
                dp[t, h] += rs1[depth + k, h] + rs2[k, h]

                @pl.when(k < depth - 1)
                def _():
                    copy_z1(k, t, h).start()

                return carry

            lax.fori_loop(0, depth, each, 0)

        def block(t, h):
            return dp_out.at[t, pl.ds(h * LANES, LANES)]

        def copy_a2(i, t, h):
            return push(block(t, h), block(t, h), as_.at[i, h], ar.at[i, h], (peer_a, c))

        def copy_b2(m, t, h):
            return push(block(t, h), block(t, h), bs.at[m, h], br.at[m, h], (peer_b, c))

        def copy_z2(k, t, h):
            return push(
                block(t, h), block(t, h), zs.at[k, h], zr.at[k, h],
                (spot(ahead(k), a, b), c),
            )

        def behind(m):
            return lax.rem(z + depth - m, depth)

        def settle(h):
            total = dp[r, h]
            for k in range(depth - 1):
                copy_z1(k, r, h).wait_recv()
                total = total + rs3[k, h]
            rows_h = pl.ds(h * LANES, LANES)
            unit, length = unit_rows(protos_in[r, rows_h])
            dp_out[r, rows_h] = unit_back(total.T, unit, length)
            copy_a2(0, r, h).start()
            copy_b2(0, r, h).start()
            for k in range(depth - 1):
                copy_z2(k, r, h).start()

        def pass_z(h):
            t = spot(z, a, 1 - b)
            copy_b2(0, t, h).wait_recv()
            copy_a2(1, t, h).start()
            for m in range(1, depth):
                t = spot(behind(m), a, b)
                copy_z2(m - 1, t, h).wait_recv()
                copy_b2(m, t, h).start()
                copy_a2(2 * m, t, h).start()

        def pass_b(h):
            for m in range(1, depth):
                t = spot(behind(m), a, 1 - b)
                copy_b2(m, t, h).wait_recv()
                copy_a2(2 * m + 1, t, h).start()

        for s in range(count + 4):
            if 2 <= s + 2 < count:
                leave_piece(s + 2)
            for lag, stage in ((4, pass_b), (3, pass_z), (2, settle), (1, hop_z), (0, hop_b)):
                if 0 <= s - lag < count:
                    stage(s - lag)

        def finish(h):
            for m in range(depth):
                copy_a2(2 * m, spot(behind(m), 1 - a, b), h).wait_recv()
                copy_a2(2 * m + 1, spot(behind(m), 1 - a, 1 - b), h).wait_recv()
            for k in range(2 * depth):
                copy_a1(k, r, h).wait_send()
                copy_a2(k, r, h).wait_send()
            for k in range(depth):
                copy_b1(k, r, h).wait_send()
                copy_b2(k, r, h).wait_send()
            for k in range(depth - 1):
                copy_z1(k, r, h).wait_send()
                copy_z2(k, r, h).wait_send()

        queries_done()
        for h in range(count):
            finish(h)

    if direct:
        spread_sent(beta, bsend, brecv)
        spread_sent(shift, hsend, hrecv)
    if not fused:
        queries_done()


def run_main(rows, cols, fused, *args):
    queries, feats = args[0].shape
    tiles, width, _ = args[1].shape
    bf16 = jnp.bfloat16
    f32 = jnp.float32
    vec = lambda *s: pltpu.VMEM(s, f32)
    sems_r = [pltpu.SemaphoreType.DMA((rows,))] * 2
    sems_c = [pltpu.SemaphoreType.DMA((cols,))] * 2
    ring = []
    if fused:
        depth = rows // 4
        cuts = width // LANES
        ring = [vec(n, cuts, feats, LANES) for n in (tiles, 2 * depth, depth, depth)]
        for count in (2, 1, 1, 2, 1, 1):
            ring += [pltpu.SemaphoreType.DMA((count * depth, cuts))] * 2
    return pl.pallas_call(
        functools.partial(main_kernel, rows, cols, fused),
        out_shape=(
            jax.ShapeDtypeStruct((tiles, width, feats) if fused else (tiles, feats, width), f32),
            jax.ShapeDtypeStruct((queries // cols, feats), f32),
        ),
        in_specs=[pl.BlockSpec(memory_space=pltpu.VMEM)] * 6,
        out_specs=(pl.BlockSpec(memory_space=pltpu.VMEM),) * 2,
        scratch_shapes=[
            pltpu.VMEM((queries, feats), bf16), pltpu.VMEM((queries, feats), bf16),
            pltpu.VMEM((tiles, width, feats), bf16), vec(tiles, 1, width),
            vec(queries, LANES), pltpu.VMEM((2, feats, queries), bf16),
            vec(tiles, queries, width), vec(tiles, queries, width),
            vec(queries, LANES), vec(queries, LANES), vec(queries, LANES), vec(queries, LANES),
            vec(cols, 2, queries),
            vec(tiles, 2, width), vec(rows, 2, width), vec(tiles, 1, width),
            vec(tiles, 1, width), vec(rows, 1, width), vec(tiles, 1, width),
            vec(1, width), vec(queries, feats),
            vec(cols, queries // cols, feats), vec(cols, 1, queries),
        ]
        + sems_c + sems_r + sems_r + sems_c + sems_r + sems_r + sems_c + ring,
        compiler_params=pltpu.CompilerParams(
            collective_id=0, has_side_effects=True, vmem_limit_bytes=56 * 1024 * 1024
        ),
        name="transport_sweeps",
    )(*args)


def hand_over(dp, dq, dp_out, dq_out, held, heldq, ins, outs):
    parts = ins.shape[0] - 1
    step = dp.shape[0] // parts
    legs = [
        (
            pltpu.make_async_copy(dq, heldq, ins.at[parts]),
            pltpu.make_async_copy(heldq, dq_out, outs.at[parts]),
        )
    ]
    for k in range(parts):
        part = pl.ds(k * step, step)
        legs.append(
            (
                pltpu.make_async_copy(dp.at[part], held.at[part], ins.at[k]),
                pltpu.make_async_copy(held.at[part], dp_out.at[part], outs.at[k]),
            )
        )
    for come, _ in legs:
        come.start()
    for come, go in legs:
        come.wait()
        go.start()
    for _, go in legs:
        go.wait()


def run_hand_over(dp, dq):
    anywhere = pl.BlockSpec(memory_space=pl.ANY)
    return pl.pallas_call(
        hand_over,
        out_shape=(
            jax.ShapeDtypeStruct(dp.shape, dp.dtype), jax.ShapeDtypeStruct(dq.shape, dq.dtype)
        ),
        in_specs=[anywhere] * 2,
        out_specs=(anywhere,) * 2,
        scratch_shapes=[
            pltpu.VMEM(dp.shape, dp.dtype), pltpu.VMEM(dq.shape, dq.dtype),
            pltpu.SemaphoreType.DMA((9,)), pltpu.SemaphoreType.DMA((9,)),
        ],
        compiler_params=pltpu.CompilerParams(vmem_limit_bytes=16 * 1024 * 1024),
        name="hand_over",
    )(dp, dq)


def local(rows, cols, queries, prototypes, potential, weights, capacity, cotangent):
    slots, feats = prototypes.shape
    width, tiles = tiles_of(slots, rows)
    fused = tiles == rows and rows % 4 == 0
    dp, dq = run_main(
        rows, cols, fused, queries, prototypes.reshape(tiles, width, feats),
        potential.reshape(tiles, 1, width), weights.reshape(1, -1),
        capacity.reshape(tiles, 1, width), cotangent,
    )
    if fused:
        grad_protos, grad_queries = run_hand_over(dp.reshape(slots, feats), dq)
        return (grad_queries, grad_protos)
    whole = lax.psum(dp, "rows")
    whole = whole.transpose(0, 2, 1).reshape(slots, feats)
    return (dq, unit_back(whole, *unit_rows(prototypes)))


def solution(mesh):
    rows, cols = mesh.shape["rows"], mesh.shape["cols"]
    in_specs = (P("rows", None), P("cols", None), P("cols"), P("rows"), P("cols"), P("rows", None))
    out_specs = (P(("rows", "cols"), None), P("cols", None))
    return jax.shard_map(
        functools.partial(local, rows, cols),
        mesh=mesh, in_specs=in_specs, out_specs=out_specs, check_vma=False,
    )
```

```python
import functools
import math

import jax
import jax.numpy as jnp
from jax import lax
from jax.experimental import pallas as pl
from jax.experimental.pallas import tpu as pltpu
from jax.sharding import PartitionSpec as P

TEMPER = 0.05
LANES = 128
MESH = pl.DeviceIdType.MESH


def unit_rows(matrix):
    wide = matrix.astype(jnp.float32)
    length = jnp.sqrt(jnp.sum(wide * wide, axis=1, keepdims=True) + 1e-06)
    return ((wide / length).astype(jnp.bfloat16), length)


def unit_back(grad, unit, length):
    wide = unit.astype(jnp.float32)
    along = jnp.sum(wide * grad, axis=1, keepdims=True)
    return (grad - wide * along) / length


def nt_dot(left, right):
    return lax.dot_general(
        left, right, (((1,), (1,)), ((), ())), preferred_element_type=jnp.float32
    )


def tiles_of(slots, rows):
    width = max(slots // rows, LANES)
    return width, slots // width


def push(src, dst, send, recv, device):
    return pltpu.make_async_remote_copy(
        src_ref=src, dst_ref=dst, send_sem=send, recv_sem=recv,
        device_id=device, device_id_type=MESH,
    )


def main_kernel(
    rows, cols, fused, queries_in, protos_in, potential, weights, capacity, cotangent,
    dp_out, dq_out, qhat, scaled, phat, offset, left_t,
    kern, coup, zacc, kacc, share, alpha, cbuf, part, pbuf, beta, gpart, gbuf, shift,
    invs, dqacc, dqbuf, rbuf, wpool, mine_q, pooled,
    csend, crecv, psend, precv, bsend, brecv, rsend, rrecv, gsend, grecv, hsend, hrecv,
    dsend, drecv, wsem, qsem, ssem, *ring,
):
    tiles, queries, width = kern.shape
    pool = 2 if fused else 1
    held = queries // pool
    group = rows // pool
    lanes = [slice(k, k + LANES) for k in range(0, width, LANES)]
    r = lax.axis_index("rows")
    c = lax.axis_index("cols")

    low = lax.rem(r // 4, 2) if fused else 0
    high = r // 8
    g = high * 4 + lax.rem(r, 4) if fused else r
    twin = r + (1 - 2 * low) * 4 if fused else r

    def row_of(u):
        return (u // 4) * 8 + low * 4 + lax.rem(u, 4) if fused else u

    barrier = pltpu.get_barrier_semaphore()
    for o in range(1, rows):
        pl.semaphore_signal(
            barrier, inc=1, device_id=(lax.rem(r + o, rows), c), device_id_type=MESH
        )
    for o in range(1, cols):
        pl.semaphore_signal(
            barrier, inc=1, device_id=(r, lax.rem(c + o, cols)), device_id_type=MESH
        )
        if fused:
            pl.semaphore_signal(
                barrier, inc=1, device_id=(twin, lax.rem(c + o, cols)), device_id_type=MESH
            )
    pl.semaphore_wait(barrier, rows - 1 + (cols - 1) * pool)

    zacc[...] = jnp.zeros_like(zacc)
    kacc[...] = jnp.zeros_like(kacc)
    dqacc[...] = jnp.zeros_like(dqacc)
    log2e = 1.0 / (TEMPER * math.log(2.0))
    step = min(held, 256)
    offset[...] = jnp.log2(capacity[...].astype(jnp.float32)) - potential[...] * log2e
    feats = qhat.shape[1]
    wide_w = weights[...].astype(jnp.float32)
    own_unit, _ = unit_rows(queries_in[...])
    tall_w = jnp.broadcast_to(wide_w, (feats, held)).T
    own_scaled = (cotangent[...].astype(jnp.float32) / tall_w).astype(jnp.bfloat16)
    wpool[low] = wide_w
    gather = []
    if fused:
        mine_q[...] = jnp.where(c == 0, own_unit.astype(jnp.float32), own_scaled.astype(jnp.float32))
        gather = [
            push(wpool.at[low], wpool.at[low], wsem.at[0], wsem.at[1], (twin, c)),
            push(mine_q, pooled.at[c], qsem.at[0], qsem.at[1], (twin, c)),
        ]
        for cp in gather:
            cp.start()

    def place(half):
        return pl.ds(pl.multiple_of(half * held, held), held)

    qhat[place(low), :] = own_unit
    scaled[place(low), :] = own_scaled

    def first(half, fresh):
        def each(t, carry):
            if fresh:
                proto, _ = unit_rows(protos_in[row_of(t)])
                phat[t] = proto
            else:
                proto = phat[t]
            base = offset[row_of(t)]
            for q in range(0, held, step):
                qs = pl.ds(pl.multiple_of(half * held + q, step), step)
                k = jnp.exp2(nt_dot(qhat[qs, :], proto) * log2e + base)
                grad = nt_dot(scaled[qs, :], proto)
                kern[t, qs, :] = k
                coup[t, qs, :] = grad
                kg = k * grad
                zsum = k[:, lanes[0]]
                gsum = kg[:, lanes[0]]
                for l in lanes[1:]:
                    zsum = zsum + k[:, l]
                    gsum = gsum + kg[:, l]
                zacc[qs, :] += zsum
                kacc[qs, :] += gsum
            return carry

        lax.fori_loop(0, tiles, each, 0)

    first(low, True)
    if fused:
        gather[1].wait()
        swap = push(pooled.at[c], pooled.at[c], ssem.at[0], ssem.at[1], (r, 1 - c))
        swap.start()
        swap.wait_send()
        other = push(pooled.at[1 - c], pooled.at[1 - c], ssem.at[0], ssem.at[1], (r, 1 - c))
        other.wait_recv()
        gather[0].wait()
        qhat[place(1 - low), :] = pooled[0].astype(jnp.bfloat16)
        scaled[place(1 - low), :] = pooled[1].astype(jnp.bfloat16)
        first(1 - low, False)
    left_t[0] = qhat[...].astype(jnp.float32).T.astype(jnp.bfloat16)
    left_t[1] = scaled[...].astype(jnp.float32).T.astype(jnp.bfloat16)

    def mates():
        for d in range(pool):
            for o in range(cols):
                if d + o > 0:
                    there = twin if d else r
                    half = 1 - low if d else low
                    yield d * cols + o, half, there, lax.rem(c + o, cols)

    def tall(row):
        return jnp.broadcast_to(row, (LANES, queries)).T

    def flat(acc):
        return jnp.sum(acc[...].T, axis=0, keepdims=True)

    def over_cols(buf, send, recv):
        copies = []
        for o, _, there, col in mates():
            cp = push(buf.at[0], buf.at[o], send.at[o], recv.at[o], (there, col))
            cp.start()
            copies.append(cp)
        for cp in copies:
            cp.wait()
        total = buf[0]
        for o in range(1, cols * pool):
            total = total + buf[o]
        return total

    cbuf[0, 0:1] = flat(zacc)
    cbuf[0, 1:2] = flat(kacc)
    total = over_cols(cbuf, csend, crecv)
    w = jnp.concatenate([wpool[k] for k in range(pool)], axis=1)
    srate = w / total[0:1]
    share[...] = tall(srate)
    alpha[...] = tall(srate * total[1:2] / w)
    direct = tiles == group

    def swept(body, part_ref, buf, send, recv):
        if not direct:
            lax.fori_loop(0, tiles, lambda t, k: body(t) or k, 0)
            scatter(part_ref, buf, send, recv)
            return

        def each(o, carry):
            t = lax.rem(g + o, group)
            body(t)

            @pl.when(o < group)
            def _():
                push(part_ref.at[t], buf.at[o], send.at[o], recv.at[o], (row_of(t), c)).start()

            return carry

        lax.fori_loop(1, group + 1, each, 0)

        def done(o, carry):
            push(part_ref.at[g], buf.at[o], send.at[o], recv.at[o], (row_of(lax.rem(g + o, group)), c)).wait()
            return carry

        lax.fori_loop(1, group, done, 0)

    def second(t):
        for l in lanes:
            p = share[...] * kern[t, :, l]
            kern[t, :, l] = p
            part[t, 0:1, l] = jnp.sum(p, axis=0, keepdims=True)
            part[t, 1:2, l] = jnp.sum(
                p * (coup[t, :, l] - alpha[...]), axis=0, keepdims=True
            )

    def scatter(src, dst, send, recv):
        def each(o, carry):
            peer = lax.rem(r + o, rows)

            def go():
                push(src.at[peer], dst.at[o], send.at[o], recv.at[o], (peer, c)).start()

            if tiles == rows:
                go()
            else:
                pl.when(peer < tiles)(go)
            return carry

        lax.fori_loop(1, rows, each, 0)

        def done(o, carry):
            peer = lax.rem(r + o, rows)

            def sent():
                push(src.at[0], dst.at[o], send.at[o], recv.at[o], (peer, c)).wait_send()

            def got():
                push(src.at[0], dst.at[o], send.at[o], recv.at[o], (peer, c)).wait_recv()

            if tiles == rows:
                sent()
                got()
            else:
                pl.when(peer < tiles)(sent)
                pl.when(r < tiles)(got)
            return carry

        lax.fori_loop(1, rows, done, 0)

    def spread_start(buf, send, recv):
        def each(o, carry):
            peer = lax.rem(g + o, group)

            def go():
                push(buf.at[g], buf.at[g], send.at[o], recv.at[o], (row_of(peer), c)).start()

            if tiles == group:
                go()
            else:
                pl.when(g < tiles)(go)
            return carry

        lax.fori_loop(1, group, each, 0)

    def spread_got(buf, send, recv, t):
        o = lax.rem(g + group - t, group)

        @pl.when(o > 0)
        def _():
            push(buf.at[t], buf.at[t], send.at[o], recv.at[o], (row_of(t), c)).wait_recv()

    def spread_sent(buf, send, recv):
        def done(o, carry):
            push(
                buf.at[g], buf.at[g], send.at[o], recv.at[o], (row_of(lax.rem(g + o, group)), c)
            ).wait_send()
            return carry

        lax.fori_loop(1, group, done, 0)

    def spread_wait(buf, send, recv):
        def done(o, carry):
            origin = lax.rem(g + group - o, group)
            peer = lax.rem(g + o, group)

            def sent():
                push(buf.at[g], buf.at[g], send.at[o], recv.at[o], (row_of(peer), c)).wait_send()

            def got():
                push(
                    buf.at[origin], buf.at[origin], send.at[o], recv.at[o], (row_of(peer), c)
                ).wait_recv()

            if tiles == group:
                sent()
                got()
            else:
                pl.when(g < tiles)(sent)
                pl.when(origin < tiles)(got)
            return carry

        lax.fori_loop(1, group, done, 0)

    def own(body):
        if tiles == group:
            body()
        else:
            pl.when(g < tiles)(body)

    swept(second, part, pbuf, psend, precv)

    def first_beta():
        both = part[g]
        for o in range(1, group):
            both = both + pbuf[o]
        inv = 1.0 / both[0:1]
        invs[...] = inv
        beta[g] = both[1:2] * inv

    own(first_beta)
    zacc[...] = jnp.zeros_like(zacc)
    spread_start(beta, bsend, brecv)
    if not direct:
        spread_wait(beta, bsend, brecv)

    def third(o, carry):
        t = o
        if direct:
            t = lax.rem(g + group - o, group)
            spread_got(beta, bsend, brecv, t)
        acc = zacc[...]
        for l in lanes:
            acc = acc + kern[t, :, l] * beta[t, :, l]
        zacc[...] = acc
        return carry

    lax.fori_loop(0, tiles, third, 0)
    rbuf[0] = flat(zacc)
    change = tall(over_cols(rbuf, rsend, rrecv) / w)
    share[...] = change
    alpha[...] = alpha[...] - change

    def fourth(t):
        for l in lanes:
            gpart[t, :, l] = jnp.sum(share[...] * kern[t, :, l], axis=0, keepdims=True)

    swept(fourth, gpart, gbuf, gsend, grecv)

    def second_beta():
        tot = gpart[g]
        for o in range(1, group):
            tot = tot + gbuf[o]
        shift[g] = beta[g] + tot * invs[...]

    own(second_beta)
    spread_start(shift, hsend, hrecv)
    if not direct:
        spread_wait(shift, hsend, hrecv)

    if fused:
        dp, rs1, rs2, rs3, s1s, s1r, s2s, s2r, s3s, s3r, as_, ar, bs, br, zs, zr = ring
    else:
        dp = dp_out

    def fifth(t):
        if direct:
            spread_got(shift, hsend, hrecv, t)
        ds = []
        pb = []
        for l in lanes:
            p = kern[t, :, l]
            ds.append(
                (p * ((coup[t, :, l] - alpha[...]) - shift[t, :, l]) * (1.0 / TEMPER)).astype(
                    jnp.bfloat16
                )
            )
            pb.append(p.astype(jnp.bfloat16))
        ds = jnp.concatenate(ds, axis=1)
        pb = jnp.concatenate(pb, axis=1)
        dqacc[...] += jnp.dot(ds, phat[t], preferred_element_type=jnp.float32)
        grad = jnp.dot(
            left_t[0], ds, preferred_element_type=jnp.float32
        ) + jnp.dot(left_t[1], pb, preferred_element_type=jnp.float32)
        if fused:
            for h, l in enumerate(lanes):
                dp[t, h] = grad[:, l]
        else:
            dp[t] = grad

    if not fused:

        def plain(t, carry):
            fifth(t)
            return carry

        lax.fori_loop(0, tiles, plain, 0)
    else:
        depth = rows // 4
        near = depth // 2
        z = r // 4
        even = lax.rem(c, 2) == 0
        wa = jnp.where(even, 1, 2)
        wb = 3 - wa
        a = jnp.where(even, lax.rem(r, 2), lax.rem(r // 2, 2))
        b = jnp.where(even, lax.rem(r // 2, 2), lax.rem(r, 2))
        peer_a = r + (1 - 2 * a) * wa
        peer_b = r + (1 - 2 * b) * wb

        def ahead_near(k):
            return lax.rem(high + 1 + k, near)

        def spot(zz, av, bv):
            return zz * 4 + av * wa + bv * wb

        def ahead(k):
            return lax.rem(z + 1 + k, depth)

        def copy_a1(i, t, h):
            return push(dp.at[t, h], rs1.at[i, h], s1s.at[i, h], s1r.at[i, h], (peer_a, c))

        def copy_b1(k, t, h):
            return push(dp.at[t, h], rs2.at[k, h], s2s.at[k, h], s2r.at[k, h], (peer_b, c))

        def copy_z1(k, t, h):
            return push(
                dp.at[t, h], rs3.at[k, h], s3s.at[k, h], s3r.at[k, h],
                (row_of(spot(ahead_near(k), a, b)), c),
            )

        def away(i):
            return spot(ahead_near(lax.rem(i, near)), 1 - a, jnp.where(i < near, 1 - b, b))

        def leave(i, carry):
            t = away(i)
            fifth(t)
            copy_a1(i, t, 0).start()
            return carry

        lax.fori_loop(0, 2 * near, leave, 0)

        def leave_piece(h):
            def each(i, carry):
                copy_a1(i, away(i), h).start()
                return carry

            lax.fori_loop(0, 2 * near, each, 0)

        leave_piece(1)

        def stay(i, carry):
            fifth(spot(ahead_near(lax.rem(i, near)), a, jnp.where(i < near, 1 - b, b)))
            return carry

        lax.fori_loop(0, 2 * near, stay, 0)

    piece = held // cols

    def piece_at(half, col):
        return pl.ds(pl.multiple_of(half * held + col * piece, piece), piece)

    copies = []
    for o, half, there, col in mates():
        cp = push(
            dqacc.at[piece_at(half, col)],
            dqbuf.at[o], dsend.at[o], drecv.at[o], (there, col),
        )
        cp.start()
        copies.append(cp)

    def queries_done():
        for cp in copies:
            cp.wait()
        mine = dqacc[piece_at(low, c), :]
        for o in range(1, cols * pool):
            mine = mine + dqbuf[o]
        unit, length = unit_rows(queries_in[piece_at(0, c), :])
        dq_out[...] = unit_back(mine, unit, length)

    if fused:
        count = len(lanes)

        def hop_b(h):
            def each(k, carry):
                t = spot(ahead_near(k), a, 1 - b)
                copy_a1(k, t, h).wait_recv()
                dp[t, h] += rs1[k, h]
                copy_b1(k, t, h).start()
                return carry

            lax.fori_loop(0, near, each, 0)

        def hop_z(h):
            def each(k, carry):
                t = spot(ahead_near(k), a, b)
                copy_a1(near + k, t, h).wait_recv()
                copy_b1(k, t, h).wait_recv()
                dp[t, h] += rs1[near + k, h] + rs2[k, h]

                @pl.when(k < near - 1)
                def _():
                    copy_z1(k, t, h).start()

                return carry

            lax.fori_loop(0, near, each, 0)

        def block(t, h):
            return dp_out.at[t, pl.ds(h * LANES, LANES)]

        def copy_a2(i, t, h):
            return push(block(t, h), block(t, h), as_.at[i, h], ar.at[i, h], (peer_a, c))

        def copy_b2(m, t, h):
            return push(block(t, h), block(t, h), bs.at[m, h], br.at[m, h], (peer_b, c))

        def copy_z2(k, t, h):
            return push(
                block(t, h), block(t, h), zs.at[k, h], zr.at[k, h],
                (spot(ahead(k), a, b), c),
            )

        def behind(m):
            return lax.rem(z + depth - m, depth)

        def settle(h):
            total = dp[g, h]
            for k in range(near - 1):
                copy_z1(k, g, h).wait_recv()
                total = total + rs3[k, h]
            rows_h = pl.ds(h * LANES, LANES)
            unit, length = unit_rows(protos_in[r, rows_h])
            dp_out[r, rows_h] = unit_back(total.T, unit, length)
            copy_a2(0, r, h).start()
            copy_b2(0, r, h).start()
            for k in range(depth - 1):
                copy_z2(k, r, h).start()

        def pass_z(h):
            t = spot(z, a, 1 - b)
            copy_b2(0, t, h).wait_recv()
            copy_a2(1, t, h).start()
            for m in range(1, depth):
                t = spot(behind(m), a, b)
                copy_z2(m - 1, t, h).wait_recv()
                copy_b2(m, t, h).start()
                copy_a2(2 * m, t, h).start()

        def pass_b(h):
            for m in range(1, depth):
                t = spot(behind(m), a, 1 - b)
                copy_b2(m, t, h).wait_recv()
                copy_a2(2 * m + 1, t, h).start()

        for s in range(count + 4):
            if 2 <= s + 2 < count:
                leave_piece(s + 2)
            for lag, stage in ((4, pass_b), (3, pass_z), (2, settle), (1, hop_z), (0, hop_b)):
                if 0 <= s - lag < count:
                    stage(s - lag)

        def finish(h):
            for m in range(depth):
                copy_a2(2 * m, spot(behind(m), 1 - a, b), h).wait_recv()
                copy_a2(2 * m + 1, spot(behind(m), 1 - a, 1 - b), h).wait_recv()
            for k in range(2 * near):
                copy_a1(k, g, h).wait_send()
            for k in range(near):
                copy_b1(k, g, h).wait_send()
            for k in range(near - 1):
                copy_z1(k, g, h).wait_send()
            for k in range(2 * depth):
                copy_a2(k, r, h).wait_send()
            for k in range(depth):
                copy_b2(k, r, h).wait_send()
            for k in range(depth - 1):
                copy_z2(k, r, h).wait_send()

        queries_done()
        for h in range(count):
            finish(h)

    if direct:
        spread_sent(beta, bsend, brecv)
        spread_sent(shift, hsend, hrecv)
    if not fused:
        queries_done()


def run_main(rows, cols, fused, *args):
    held, feats = args[0].shape
    total, width, _ = args[1].shape
    pool = 2 if fused else 1
    queries, tiles, group = held * pool, total // pool, rows // pool
    mates = cols * pool
    bf16 = jnp.bfloat16
    f32 = jnp.float32
    vec = lambda *s: pltpu.VMEM(s, f32)
    sems_r = [pltpu.SemaphoreType.DMA((group,))] * 2
    sems_c = [pltpu.SemaphoreType.DMA((mates,))] * 2
    ring = []
    if fused:
        depth = rows // 4
        near = depth // 2
        cuts = width // LANES
        ring = [vec(n, cuts, feats, LANES) for n in (tiles, 2 * near, near, near)]
        for count in (2 * near, near, near, 2 * depth, depth, depth):
            ring += [pltpu.SemaphoreType.DMA((count, cuts))] * 2
    return pl.pallas_call(
        functools.partial(main_kernel, rows, cols, fused),
        out_shape=(
            jax.ShapeDtypeStruct((total, width, feats) if fused else (total, feats, width), f32),
            jax.ShapeDtypeStruct((held // cols, feats), f32),
        ),
        in_specs=[pl.BlockSpec(memory_space=pltpu.VMEM)] * 6,
        out_specs=(pl.BlockSpec(memory_space=pltpu.VMEM),) * 2,
        scratch_shapes=[
            pltpu.VMEM((queries, feats), bf16), pltpu.VMEM((queries, feats), bf16),
            pltpu.VMEM((tiles, width, feats), bf16), vec(total, 1, width),
            pltpu.VMEM((2, feats, queries), bf16),
            vec(tiles, queries, width), vec(tiles, queries, width),
            vec(queries, LANES), vec(queries, LANES), vec(queries, LANES), vec(queries, LANES),
            vec(mates, 2, queries),
            vec(tiles, 2, width), vec(group, 2, width), vec(tiles, 1, width),
            vec(tiles, 1, width), vec(group, 1, width), vec(tiles, 1, width),
            vec(1, width), vec(queries, feats),
            vec(mates, held // cols, feats), vec(mates, 1, queries),
            vec(pool, 1, held), vec(held, feats), vec(2, held, feats),
        ]
        + sems_c + sems_r + sems_r + sems_c + sems_r + sems_r + sems_c + [pltpu.SemaphoreType.DMA((2,))] * 3 + ring,
        compiler_params=pltpu.CompilerParams(
            collective_id=0, has_side_effects=True, vmem_limit_bytes=56 * 1024 * 1024
        ),
        name="transport_sweeps",
    )(*args)


def hand_over(dp, dq, dp_out, dq_out, held, heldq, ins, outs):
    parts = ins.shape[0] - 1
    step = dp.shape[0] // parts
    legs = [
        (
            pltpu.make_async_copy(dq, heldq, ins.at[parts]),
            pltpu.make_async_copy(heldq, dq_out, outs.at[parts]),
        )
    ]
    for k in range(parts):
        part = pl.ds(k * step, step)
        legs.append(
            (
                pltpu.make_async_copy(dp.at[part], held.at[part], ins.at[k]),
                pltpu.make_async_copy(held.at[part], dp_out.at[part], outs.at[k]),
            )
        )
    for come, _ in legs:
        come.start()
    for come, go in legs:
        come.wait()
        go.start()
    for _, go in legs:
        go.wait()


def run_hand_over(dp, dq):
    anywhere = pl.BlockSpec(memory_space=pl.ANY)
    return pl.pallas_call(
        hand_over,
        out_shape=(
            jax.ShapeDtypeStruct(dp.shape, dp.dtype), jax.ShapeDtypeStruct(dq.shape, dq.dtype)
        ),
        in_specs=[anywhere] * 2,
        out_specs=(anywhere,) * 2,
        scratch_shapes=[
            pltpu.VMEM(dp.shape, dp.dtype), pltpu.VMEM(dq.shape, dq.dtype),
            pltpu.SemaphoreType.DMA((9,)), pltpu.SemaphoreType.DMA((9,)),
        ],
        compiler_params=pltpu.CompilerParams(vmem_limit_bytes=56 * 1024 * 1024),
        name="hand_over",
    )(dp, dq)


def local(rows, cols, queries, prototypes, potential, weights, capacity, cotangent):
    slots, feats = prototypes.shape
    width, tiles = tiles_of(slots, rows)
    fused = tiles == rows and rows % 8 == 0 and cols == 2
    dp, dq = run_main(
        rows, cols, fused, queries, prototypes.reshape(tiles, width, feats),
        potential.reshape(tiles, 1, width), weights.reshape(1, -1),
        capacity.reshape(tiles, 1, width), cotangent,
    )
    if fused:
        grad_protos, grad_queries = run_hand_over(dp.reshape(slots, feats), dq)
        return (grad_queries, grad_protos)
    whole = lax.psum(dp, "rows")
    whole = whole.transpose(0, 2, 1).reshape(slots, feats)
    return (dq, unit_back(whole, *unit_rows(prototypes)))


def solution(mesh):
    rows, cols = mesh.shape["rows"], mesh.shape["cols"]
    in_specs = (P("rows", None), P("cols", None), P("cols"), P("rows"), P("cols"), P("rows", None))
    out_specs = (P(("rows", "cols"), None), P("cols", None))
    return jax.shard_map(
        functools.partial(local, rows, cols),
        mesh=mesh, in_specs=in_specs, out_specs=out_specs, check_vma=False,
    )
```
